768 devices in a mesh: ax: 12 (over z), cr: 64 (over y, x, core).
Axes of the slice: x: 4, y: 8, z: 12, core: 2. Of those that a mesh axis runs over, the one named last changes fastest.
Arguments:
- parcels: bfloat16 [12, 64, 64, 16, 64], P('ax', 'cr'), may hold values from -6 to 6
- cell_index: int32 [12, 64, 64, 64], P('ax', 'cr'), may hold values from 0 to 131071
- counts: int32 [12, 64, 64], P('ax', 'cr'), may hold values from 0 to 64, as said below
- coupling: bfloat16 [4, 16], replicated, may hold values from -1.5 to 1.5
Outputs:
- smoothed: float32 [4, 384, 2048, 128], P(None, 'ax', 'cr')
The draws below stay inside these ranges and needn't reach their ends.
Inputs may be any that keep to these rules, and one draw needn't show every extreme that they name: The live slots of a bucket are its first counts[a, c, d]; in every draw some brick receives 64 live parcels from each brick of its slab.
All inputs are finite; a program needn't handle non-finite values.
Results may differ from the reference program's by a relative error of at most 0.0029.
Values may be sent and summed in bfloat16 or wider, within the bound.
A program may use at most 32 MiB of HBM per device.

```python
import math
import jax
import jax.numpy as jnp
from jax import lax

CA = 32
CY = 32
NZ = 128
CAP = 64
FEAT = 16
COMP = 4
HALF = 16
NX = 384
NY = 2048
CELLS = 131072
N_AX = 12
N_CR = 64


def draw_counts(key, part):
    slab_key, wall_key, spread_key, throat_key, cycle_key = jax.random.split(key, 5)
    slab_load = jax.random.randint(slab_key, (N_AX,), 1, 5)
    throat = jax.random.randint(throat_key, (), 0, N_AX)
    slab_load = jnp.where(jnp.arange(N_AX, dtype=jnp.int32) == throat, 4, slab_load)
    wall_load = jax.random.randint(wall_key, (N_CR,), 1, 5)
    hottest = jax.random.randint(cycle_key, (), 0, N_CR)
    wall_load = jnp.where(jnp.arange(N_CR, dtype=jnp.int32) == hottest, 4, wall_load)
    spread = jax.random.randint(spread_key, (N_AX, N_CR, N_CR), 0, CAP + 1)
    load = slab_load[:, None, None] * wall_load[None, None, :]
    result = jnp.minimum(CAP, spread * load // 8)
    result = jnp.where(load == 16, CAP, result)
    return result.astype(jnp.int32)


def with_ends(entries, key, low, high):
    longest = entries.shape.index(max(entries.shape))
    spots = []
    for shift in (0, 1):
        where = [jax.random.randint(jax.random.fold_in(key, axis), (), 0, length) for axis, length in enumerate(entries.shape)]
        where[longest] = (where[longest] + shift) % entries.shape[longest]
        spots.append(tuple(where))
    return entries.at[spots[0]].set(low).at[spots[1]].set(high)


def block_scale(rng, shape, pieces, smallest, high):
    level, own = 1.0, jax.random.fold_in(rng, 6)
    for position, shards_of in pieces:
        draws = jnp.exp(jax.random.uniform(jax.random.fold_in(own, position), (shards_of,), jnp.float32, smallest / len(pieces), high / len(pieces)))
        level = level * jnp.repeat(draws, shape[position] // shards_of).reshape([-1 if axis == position else 1 for axis in range(len(shape))])
    return level


def centred(rng, shape, deviation, limit, shards=(), held_as=jnp.bfloat16):
    level = block_scale(rng, shape, shards, -0.22, 0.18) if shards else 1.0
    entries = jax.random.normal(rng, shape, jnp.float32) * deviation * level
    return jnp.minimum(jnp.maximum(entries, -limit), limit).astype(held_as)


def setup_inputs(seed: int = 0) -> dict:
    key_list = jax.random.split(jax.random.key(seed), 5)
    return {
        "parcels": centred(key_list[0], (N_AX, N_CR, N_CR, FEAT, CAP), 1.0, 6.0, ((0, 12), (1, 64))),
        "cell_index": with_ends(jax.random.randint(key_list[1], (N_AX, N_CR, N_CR, CAP), 0, CELLS), jax.random.fold_in(key_list[1], 1), 0, CELLS - 1).astype(jnp.int32),
        "counts": draw_counts(jax.random.fold_in(key_list[4], 71), 0),
        "coupling": centred(key_list[3], (COMP, FEAT), FEAT ** -0.5, 1.5),
    }


volume_inv = 256.0
sigma_ratio = 0.75


def band_matrix(count_out, count_in, first_out, first_in, extent):
    sigma = sigma_ratio * HALF
    out_pos = first_out + jnp.arange(count_out, dtype=jnp.int32)
    in_pos = first_in + jnp.arange(count_in, dtype=jnp.int32)
    spacing = in_pos[None, :] - out_pos[:, None]
    spacing_f = spacing.astype(jnp.float32)
    kernel = jnp.where(jnp.abs(spacing) <= HALF, jnp.exp(-spacing_f * spacing_f / (2.0 * sigma * sigma)), 0.0)
    offsets = jnp.arange(-HALF, HALF + 1, dtype=jnp.int32)
    offsets_f = offsets.astype(jnp.float32)
    tap_values = jnp.exp(-offsets_f * offsets_f / (2.0 * sigma * sigma))
    reach = out_pos[:, None] + offsets[None, :]
    inside = (reach >= 0) & (reach < extent)
    weight_sum = jnp.sum(jnp.where(inside, tap_values[None, :], 0.0), axis=1)
    return kernel / weight_sum[:, None]


def smooth_shifted(fields, axis):
    extent = fields.shape[axis]
    sigma = sigma_ratio * HALF
    pad_widths = tuple((HALF, HALF) if number == axis else (0, 0) for number in range(fields.ndim))
    padded = jnp.pad(fields, pad_widths)
    running = jnp.zeros_like(fields)
    positions = jnp.arange(extent, dtype=jnp.int32)
    weight_sum = jnp.zeros((extent,), jnp.float32)
    for offset in range(-HALF, HALF + 1):
        tap_value = math.exp(-offset * offset / (2.0 * sigma * sigma))
        running = running + tap_value * lax.slice_in_dim(padded, offset + HALF, offset + HALF + extent, axis=axis)
        inside = (positions + offset >= 0) & (positions + offset < extent)
        weight_sum = weight_sum + jnp.where(inside, tap_value, 0.0)
    target = tuple(extent if number == axis else 1 for number in range(fields.ndim))
    return running / weight_sum.reshape(target)


def reference(parcels, cell_index, counts, coupling):
    slot_ids = jnp.arange(CAP, dtype=jnp.int32)
    live_mask = (slot_ids[None, None, None, :] < counts[:, :, :, None]).astype(jnp.bfloat16)
    sources = jnp.einsum("fj,acdjk->acdfk", coupling.astype(jnp.float32), parcels.astype(jnp.float32))
    sources = sources.astype(jnp.bfloat16) * live_mask[:, :, :, None, :]
    slab_ids = jnp.arange(N_AX, dtype=jnp.int32)[:, None, None, None]
    brick_ids = jnp.arange(N_CR, dtype=jnp.int32)[None, None, :, None]
    axial_pos = slab_ids * CA + cell_index // (CY * NZ)
    cross_pos = brick_ids * CY + (cell_index // NZ) % CY
    depth_pos = cell_index % NZ
    flat_index = ((axial_pos * NY + cross_pos) * NZ + depth_pos).reshape(-1)
    values = jnp.moveaxis(sources, 3, 0).reshape(COMP, -1).astype(jnp.float32)
    fields = jnp.zeros((COMP, NX * NY * NZ), jnp.float32).at[:, flat_index].add(values)
    fields = fields.reshape(COMP, NX, NY, NZ)
    band_depth = band_matrix(NZ, NZ, 0, 0, NZ)
    fields = jnp.einsum("fxyz,wz->fxyw", fields, band_depth, precision=lax.Precision.HIGHEST)
    band_axial = band_matrix(NX, NX, 0, 0, NX)
    fields = jnp.einsum("fxyz,wx->fwyz", fields, band_axial, precision=lax.Precision.HIGHEST)
    fields = smooth_shifted(fields, 2)
    return volume_inv * fields
```

```python
import math

import jax
import jax.numpy as jnp
import ml_dtypes
import numpy as np
from jax import lax
from jax.experimental import pallas as pl
from jax.experimental.pallas import tpu as pltpu
from jax.sharding import PartitionSpec as P

CA = 32
CY = 32
NZ = 128
COMP = 4
HALF = 16
NX = 384
NY = 2048
SLOTS = 4096
FZ = COMP * NZ
BF = jnp.bfloat16
F32 = jnp.float32
NT = (((1,), (1,)), ((), ()))

VOLUME = 256.0
SIGMA = 0.75 * HALF
TAPS = [math.exp(-k * k / (2.0 * SIGMA * SIGMA)) for k in range(HALF + 1)]
STRETCH = 1.8433
HELD = [float(np.float32(STRETCH * t).astype(ml_dtypes.bfloat16)) for t in TAPS]
_W = [1.0] + [2.0] * HALF
UNDO = sum(w * h * t for w, h, t in zip(_W, HELD, TAPS)) / sum(w * h * h for w, h in zip(_W, HELD))


def band(out_pos, in_pos):
    gap = np.abs(np.asarray(in_pos)[None, :] - np.asarray(out_pos)[:, None])
    held = np.asarray(HELD + [0.0], np.float32)
    return held[np.minimum(gap, HALF + 1)]


OWN, BELOW, ABOVE = np.arange(32), np.arange(-16, 0), np.arange(32, 48)
ROWS = 16


def _kx():
    pieces = []
    for p in (OWN, BELOW, ABOVE):
        b = band(OWN, p)
        n = b.shape[1]
        m = np.zeros((32, 8, 8, n), np.float32)
        for y in range(8):
            m[:, y, y, :] = b
        pieces.append(m.reshape(256, 8 * n))
    return np.concatenate(pieces, axis=1).astype(ml_dtypes.bfloat16)


def _ky():
    eye = np.eye(4, dtype=np.float32)
    return np.concatenate([np.kron(eye, band(OWN, p)) for p in (OWN, BELOW, ABOVE)], axis=1).astype(ml_dtypes.bfloat16)


def _kz():
    b = band(np.arange(NZ), np.arange(NZ)).T
    return np.concatenate([b, b], axis=0).astype(ml_dtypes.bfloat16)


def deposit_kernel(own_ref, below_ref, above_ref, kx_ref, e_ref, wt, acc):
    lists = (own_ref, below_ref, above_ref)
    one, zero = jnp.ones((), BF), jnp.zeros((), BF)

    def rows_iota(n, width):
        return lax.broadcasted_iota(jnp.int32, (n, width), 0).astype(F32).astype(BF)

    width = 1024
    for l, ref in enumerate(lists):
        for b in range(SLOTS // width):
            ks = pl.ds(b * width, width)
            hit = jnp.broadcast_to(ref[4:5, ks], (NZ, width)) == rows_iota(NZ, width)
            for f in range(COMP):
                s = jnp.broadcast_to(ref[f : f + 1, ks], (NZ, width))
                wt[l, f * NZ : (f + 1) * NZ, ks] = jnp.where(hit, s, zero)
    for c in range(CY // ROWS):
        for l, ref in enumerate(lists):
            n = 32 if l == 0 else 16
            x0 = (0, 16, 0)[l]
            r0 = (0, ROWS * 32, ROWS * 48)[l]
            y = ref[5:6, :].astype(F32) - float(c * ROWS)
            x = ref[6:7, :].astype(F32) - float(x0)
            ok = (x >= 0) & (x < n)
            parts = []
            for i in range(ROWS):
                key = jnp.where(ok & (y == i), x, -1.0).astype(BF)
                parts.append(jnp.where(jnp.broadcast_to(key, (n, SLOTS)) == rows_iota(n, SLOTS), one, zero))
            picks = jnp.concatenate(parts, axis=0)
            acc[r0 : r0 + ROWS * n, :] = lax.dot_general(picks, wt[l], NT, preferred_element_type=F32)
        done = []
        for i in range(ROWS // 8):
            d = jnp.concatenate(
                [
                    acc[i * 256 : (i + 1) * 256, :],
                    acc[ROWS * 32 + i * 128 : ROWS * 32 + (i + 1) * 128, :],
                    acc[ROWS * 48 + i * 128 : ROWS * 48 + (i + 1) * 128, :],
                ],
                axis=0,
            )
            high = d.astype(BF)
            low = (d - high.astype(F32)).astype(BF)
            r = jnp.dot(kx_ref[...], high, preferred_element_type=F32)
            r += jnp.dot(kx_ref[...], low, preferred_element_type=F32)
            done.append(r.reshape(CA, 8, FZ))
        e_ref[:, c * ROWS : (c + 1) * ROWS, :] = jnp.concatenate(done, axis=1).astype(BF)


def weight_sum(pos, extent):
    total = jnp.zeros(pos.shape, F32)
    for k in range(-HALF, HALF + 1):
        inside = (pos + k >= 0) & (pos + k < extent)
        total = total + jnp.where(inside, TAPS[abs(k)], 0.0)
    return total


def finish_kernel(at_ref, own_ref, below_ref, above_ref, ky_ref, kz_ref, out_ref):
    step = pl.program_id(0)
    layers = own_ref.shape[0]
    pos_z = lax.broadcasted_iota(jnp.int32, (8, NZ), 1)
    pos_y = lax.broadcasted_iota(jnp.int32, (CY, NZ), 0) + at_ref[1] * CY
    yz = (weight_sum(pos_y, NY) * weight_sum(pos_z, NZ)[0:1, :])
    for g in range(layers // 4):
        xs = slice(g * 4, g * 4 + 4)
        rhs = jnp.concatenate(
            [
                own_ref[xs].reshape(128, FZ),
                below_ref[xs].reshape(64, FZ),
                above_ref[xs].reshape(64, FZ),
            ],
            axis=0,
        )
        v = jnp.dot(ky_ref[...], rhs, preferred_element_type=F32)
        v = jnp.concatenate([v[:, f * NZ : (f + 1) * NZ] for f in range(COMP)], axis=0)
        high = v.astype(BF)
        low = (v - high.astype(F32)).astype(BF)
        r = jnp.dot(jnp.concatenate([high, low], axis=1), kz_ref[...], preferred_element_type=F32)
        pos_x = lax.broadcasted_iota(jnp.int32, (4, 8, NZ), 0) + (at_ref[0] * CA + step * layers + g * 4)
        scale = (VOLUME * UNDO**3) / (weight_sum(pos_x, NX)[:, 0:1, :] * yz[None])
        for f in range(COMP):
            out_ref[f, xs] = r[f * 128 : (f + 1) * 128].reshape(4, CY, NZ) * scale


VMEM_SPEC = pl.BlockSpec(memory_space=pltpu.VMEM)
LAYERS = 8


def on_device(parcels, cell_index, counts, coupling):
    bricks = lax.axis_size("cr")
    slabs = lax.axis_size("ax")
    capacity = parcels.shape[-1]
    slot_ids = jnp.arange(capacity, dtype=jnp.int32)
    live = slot_ids[None, :] < counts[0, 0][:, None]
    sources = jnp.einsum("fj,sjk->sfk", coupling, parcels[0, 0], preferred_element_type=F32)
    sources = jnp.where(live[:, None, :], sources.astype(BF), jnp.zeros((), BF))
    cell = cell_index[0, 0][:, None, :]
    places = jnp.concatenate([cell % NZ, (cell // NZ) % CY, cell // (NZ * CY), cell * 0], axis=1).astype(F32).astype(BF)
    letters = jnp.concatenate([sources, places], axis=1)
    arrived = lax.all_to_all(letters, "cr", split_axis=0, concat_axis=0, tiled=True)
    own = arrived.transpose(1, 0, 2).reshape(8, SLOTS)
    below = lax.ppermute(own, "ax", [(i, i + 1) for i in range(slabs - 1)])
    above = lax.ppermute(own, "ax", [(i + 1, i) for i in range(slabs - 1)])
    fields = pl.pallas_call(
        deposit_kernel,
        out_shape=jax.ShapeDtypeStruct((CA, CY, FZ), BF),
        in_specs=[VMEM_SPEC] * 4,
        out_specs=VMEM_SPEC,
        scratch_shapes=[pltpu.VMEM((3, FZ, SLOTS), BF), pltpu.VMEM((ROWS * 64, FZ), F32)],
        compiler_params=pltpu.CompilerParams(vmem_limit_bytes=60 << 20),
        name="deposit",
    )(own, below, above, jnp.asarray(_kx()))
    left = lax.ppermute(fields[:, 16:], "cr", [(i, i + 1) for i in range(bricks - 1)])
    right = lax.ppermute(fields[:, :16], "cr", [(i + 1, i) for i in range(bricks - 1)])
    at = jnp.stack([lax.axis_index("ax"), lax.axis_index("cr")]).astype(jnp.int32)
    return pl.pallas_call(
        finish_kernel,
        grid=(CA // LAYERS,),
        out_shape=jax.ShapeDtypeStruct((COMP, CA, CY, NZ), F32),
        in_specs=[
            pl.BlockSpec(memory_space=pltpu.SMEM),
            pl.BlockSpec((LAYERS, CY, FZ), lambda i: (i, 0, 0)),
            pl.BlockSpec((LAYERS, 16, FZ), lambda i: (i, 0, 0)),
            pl.BlockSpec((LAYERS, 16, FZ), lambda i: (i, 0, 0)),
            pl.BlockSpec((128, 256), lambda i: (0, 0)),
            pl.BlockSpec((256, NZ), lambda i: (0, 0)),
        ],
        out_specs=pl.BlockSpec((COMP, LAYERS, CY, NZ), lambda i: (0, i, 0, 0)),
        compiler_params=pltpu.CompilerParams(vmem_limit_bytes=40 << 20),
        name="finish",
    )(at, fields, left, right, jnp.asarray(_ky()), jnp.asarray(_kz()))


def solution(mesh):
    return jax.shard_map(
        on_device,
        mesh=mesh,
        in_specs=(
            P("ax", "cr", None, None, None),
            P("ax", "cr", None, None),
            P("ax", "cr", None),
            P(),
        ),
        out_specs=P(None, "ax", "cr", None),
        check_vma=False,
    )
```

```python
import math

import jax
import jax.numpy as jnp
import ml_dtypes
import numpy as np
from jax import lax
from jax.experimental import pallas as pl
from jax.experimental.pallas import tpu as pltpu
from jax.sharding import PartitionSpec as P

CA = 32
CY = 32
NZ = 128
COMP = 4
HALF = 16
NX = 384
NY = 2048
SLOTS = 4096
FZ = COMP * NZ
BF = jnp.bfloat16
F32 = jnp.float32
NT = (((1,), (1,)), ((), ()))

VOLUME = 256.0
SIGMA = 0.75 * HALF
TAPS = [math.exp(-k * k / (2.0 * SIGMA * SIGMA)) for k in range(HALF + 1)]
STRETCH = 1.8433
HELD = [float(np.float32(STRETCH * t).astype(ml_dtypes.bfloat16)) for t in TAPS]
_W = [1.0] + [2.0] * HALF
UNDO = sum(w * h * t for w, h, t in zip(_W, HELD, TAPS)) / sum(w * h * h for w, h in zip(_W, HELD))


def band(out_pos, in_pos):
    gap = np.abs(np.asarray(in_pos)[None, :] - np.asarray(out_pos)[:, None])
    held = np.asarray(HELD + [0.0], np.float32)
    return held[np.minimum(gap, HALF + 1)]


OWN, BELOW, ABOVE = np.arange(32), np.arange(-16, 0), np.arange(32, 48)
ROWS = 16


def _kx():
    pieces = []
    for p in (OWN, BELOW, ABOVE):
        b = band(OWN, p)
        n = b.shape[1]
        m = np.zeros((32, 8, 8, n), np.float32)
        for y in range(8):
            m[:, y, y, :] = b
        pieces.append(m.reshape(256, 8 * n))
    return np.concatenate(pieces, axis=1).astype(ml_dtypes.bfloat16)


def _ky():
    eye = np.eye(4, dtype=np.float32)
    parts = (OWN[:16], OWN[16:], BELOW, ABOVE)
    return np.concatenate([np.kron(eye, band(OWN, p)) for p in parts], axis=1).astype(ml_dtypes.bfloat16)


def _kz():
    b = band(np.arange(NZ), np.arange(NZ)).T
    return np.concatenate([b, b], axis=0).astype(ml_dtypes.bfloat16)


def iota(shape, axis):
    return lax.broadcasted_iota(jnp.int32, shape, axis)


def weight_sum(pos, extent):
    total = jnp.zeros(pos.shape, F32)
    for k in range(-HALF, HALF + 1):
        inside = (pos + k >= 0) & (pos + k < extent)
        total = total + jnp.where(inside, TAPS[abs(k)], 0.0)
    return total


def split(v):
    high = v.astype(BF)
    return high, (v - high.astype(F32)).astype(BF)


def whole_kernel(
    parcels_ref, cell_ref, counts_ref, coupling_ref, kx_ref, ky_ref, kz_ref, out_ref,
    msg1, buf1, msg2, lists, flat, wt, picks, acc_own, acc_side, e_own, e_side, kxs, kys, sx, syz,
    send1, recv1, send2, recv2, send_ax, recv_ax, send_cr, recv_cr,
):
    a, c_at = lax.axis_index("ax"), lax.axis_index("cr")
    n_ax, n_cr = lax.axis_size("ax"), lax.axis_size("cr")
    y_at, g_at = c_at // 8, c_at % 8
    up, down = lax.rem(a + 1, n_ax), lax.rem(a + n_ax - 1, n_ax)
    right, left = lax.rem(c_at + 1, n_cr), lax.rem(c_at + n_cr - 1, n_cr)
    in_row = [(a, y_at * 8 + lax.rem(g_at + j, 8)) for j in range(1, 8)]
    in_column = [(a, lax.rem(y_at + j, 8) * 8 + g_at) for j in range(1, 8)]

    def remote(src, dst, send, recv, to):
        return pltpu.make_async_remote_copy(
            src_ref=src, dst_ref=dst, send_sem=send, recv_sem=recv, device_id=to, device_id_type=pl.DeviceIdType.MESH
        )

    barrier = pltpu.get_barrier_semaphore()
    partners = in_row + in_column + [(up, c_at), (down, c_at), (a, right), (a, left)]
    for to in partners:
        pl.semaphore_signal(barrier, inc=1, device_id=to, device_id_type=pl.DeviceIdType.MESH)

    one, zero = jnp.ones((), BF), jnp.zeros((), BF)

    r, s = iota((128, 4), 0), iota((128, 4), 1)
    spread = jnp.dot(((r & 7) == s).astype(F32).astype(BF), coupling_ref[...], preferred_element_type=F32).astype(BF)
    r, s = iota((16, 256), 0), iota((16, 256), 1)
    spread = jnp.dot(spread, ((s & 15) == r).astype(F32).astype(BF), preferred_element_type=F32)
    r, s = iota((128, 256), 0), iota((128, 256), 1)
    mix = jnp.where((r >> 3) == (s >> 4), spread, 0.0).astype(BF)
    eye = (iota((64, 64), 0) == iota((64, 64), 1)).astype(F32).astype(BF)
    counts = jnp.broadcast_to(counts_ref[...].astype(F32), (64, 64)).astype(BF)
    counts = lax.dot_general(eye, counts, NT, preferred_element_type=F32)
    live = iota((64, 64), 1).astype(F32) < counts
    cell = cell_ref[...]
    codes = []
    for code in (jnp.where(live, cell & 127, -1), (cell >> 7) & 31, cell >> 12):
        code = code.astype(F32)
        codes.append(jnp.concatenate([code[:32], code[32:]], axis=1))
    codes = jnp.concatenate(codes, axis=0).astype(BF)
    for group in range(2):
        records = []
        for b in range(16):
            d = (b % 4) * 8 + 4 * group + b // 4
            records.append(jnp.concatenate([parcels_ref[d], parcels_ref[d + 32]], axis=1))
        letter = jnp.dot(mix, jnp.concatenate(records, axis=0), preferred_element_type=F32)
        r, s = iota((128, 96), 0), iota((128, 96), 1)
        b = r >> 3
        choose = ((r & 7) == 4 + (s >> 5)) & ((s & 31) == (b & 3) * 8 + 4 * group + (b >> 2))
        letter += jnp.dot(choose.astype(F32).astype(BF), codes, preferred_element_type=F32)
        msg1[group * 4 : group * 4 + 4] = letter.astype(BF).reshape(4, 32, 128)

    pl.semaphore_wait(barrier, len(partners))
    first = []
    for j in range(1, 8):
        first.append(remote(msg1.at[lax.rem(g_at + j, 8)], buf1.at[g_at], send1.at[j - 1], recv1.at[j - 1], in_row[j - 1]))
        first[-1].start()
    buf1[g_at] = msg1[g_at]

    col = iota((256, 512), 1)
    gone = ((a == 0) & (col >= 256) & (col < 384)) | ((a == n_ax - 1) & (col >= 384))
    kxs[...] = jnp.where(gone, 0.0, kx_ref[...].astype(F32)).astype(BF)
    col = iota((128, 256), 1)
    gone = ((c_at == 0) & (col >= 128) & (col < 192)) | ((c_at == n_cr - 1) & (col >= 192))
    kys[...] = jnp.where(gone, 0.0, ky_ref[...].astype(F32)).astype(BF)
    sx[...] = 1.0 / weight_sum(iota((CA, NZ), 0) + a * CA, NX)
    syz[...] = (VOLUME * UNDO**3) / (
        weight_sum(iota((CY, NZ), 0) + c_at * CY, NY) * weight_sum(iota((8, NZ), 1), NZ)[0:1, :]
    )

    for copy in first:
        copy.wait_recv()
    near = iota((32, 128), 1) < 64
    halves = []
    for m in range(4):
        p, q = buf1[2 * m].astype(F32), buf1[2 * m + 1].astype(F32)
        halves.append((jnp.where(near, p, pltpu.roll(q, 64, 1)), jnp.where(near, pltpu.roll(p, 64, 1), q)))
    for h in range(2):
        for i in range(4):
            msg2[4 * h + i] = jnp.concatenate([halves[m][h][i * 8 : i * 8 + 8] for m in range(4)], axis=0).astype(BF)
    second = []
    for j in range(1, 8):
        second.append(
            remote(
                msg2.at[lax.rem(y_at + j, 8)], lists.at[0, y_at], send2.at[j - 1], recv2.at[j - 1], in_column[j - 1]
            )
        )
        second[-1].start()
    lists[0, y_at] = msg2[y_at]
    for copy in second:
        copy.wait_recv()
    along = [
        remote(lists.at[0], lists.at[1], send_ax.at[0], recv_ax.at[0], (up, c_at)),
        remote(lists.at[0], lists.at[2], send_ax.at[1], recv_ax.at[1], (down, c_at)),
    ]
    for copy in along:
        copy.start()

    def rows_iota(n, width):
        return iota((n, width), 0).astype(F32).astype(BF)

    def unfold(l):
        rows = lists[l].astype(F32).reshape(256, 128)
        flat[l] = jnp.concatenate([rows[b * 8 : b * 8 + 8] for b in range(32)], axis=1)
        width = 1024
        for b in range(SLOTS // width):
            ks = pl.ds(b * width, width)
            hit = jnp.broadcast_to(flat[l, 4:5, ks].astype(BF), (NZ, width)) == rows_iota(NZ, width)
            for f in range(COMP):
                source = jnp.broadcast_to(flat[l, f : f + 1, ks].astype(BF), (NZ, width))
                wt[l, f * NZ : (f + 1) * NZ, ks] = jnp.where(hit, source, zero)

    def picked(l, c):
        n, x0 = (32, 0) if l == 0 else (16, 16 if l == 1 else 0)
        y = flat[l, 5:6, :] - float(c * ROWS)
        x = flat[l, 6:7, :] - float(x0)
        ok = (x >= 0) & (x < n)
        parts = []
        for i in range(ROWS):
            key = jnp.where(ok & (y == i), x, -1.0).astype(BF)
            parts.append(jnp.where(jnp.broadcast_to(key, (n, SLOTS)) == rows_iota(n, SLOTS), one, zero))
        return jnp.concatenate(parts, axis=0)

    unfold(0)
    for c in range(2):
        acc_own[c] = lax.dot_general(picked(0, c), wt[0], NT, preferred_element_type=F32)
    for l in (1, 2):
        along[l - 1].wait_recv()
        unfold(l)
    across = []
    for h in range(2):
        fs = slice(h * 256, h * 256 + 256)
        for c in range(2):
            for l in (1, 2):
                if h == 0:
                    picks[c, l - 1] = picked(l, c)
                acc_side[l - 1] = lax.dot_general(picks[c, l - 1], wt[l, fs, :], NT, preferred_element_type=F32)
            done = []
            for i in range(2):
                own = acc_own[c, i * 256 : i * 256 + 256, fs]
                sides = [acc_side[k, i * 128 : i * 128 + 128, :] for k in range(2)]
                high, low = split(jnp.concatenate([own] + sides, axis=0))
                v = jnp.dot(kxs[...], high, preferred_element_type=F32)
                v += jnp.dot(kxs[...], low, preferred_element_type=F32)
                done.append(v.reshape(CA, 8, 256))
            e_own[h, c] = jnp.concatenate(done, axis=1).astype(BF)
            k = h * 2 + c
            across.append(remote(e_own.at[h, c], e_side.at[h, 1 - c], send_cr.at[k], recv_cr.at[k], (a, (left, right)[c])))
            across[-1].start()
    for h in range(2):
        across[2 * h].wait_recv()
        across[2 * h + 1].wait_recv()

        def layers(g, _):
            xs = pl.ds(g * 4, 4)
            rhs = [e_own[h, c, xs].reshape(64, 256) for c in range(2)] + [e_side[h, c, xs].reshape(64, 256) for c in range(2)]
            v = jnp.dot(kys[...], jnp.concatenate(rhs, axis=0), preferred_element_type=F32)
            high, low = split(jnp.concatenate([v[:, :128], v[:, 128:]], axis=0))
            v = jnp.dot(jnp.concatenate([high, low], axis=1), kz_ref[...], preferred_element_type=F32)
            v = v.reshape(2, 4, CY, NZ)
            for i in range(4):
                scale = syz[...] * sx[pl.ds(g * 4 + i, 1), :]
                for f in range(2):
                    out_ref[2 * h + f, g * 4 + i] = v[f, i] * scale
            return 0

        lax.fori_loop(0, CA // 4, layers, 0)
    for copy in first + second + along + across:
        copy.wait_send()


VMEM_SPEC = pl.BlockSpec(memory_space=pltpu.VMEM)


def on_device(parcels, cell_index, counts, coupling):
    return pl.pallas_call(
        whole_kernel,
        out_shape=jax.ShapeDtypeStruct((COMP, CA, CY, NZ), F32),
        in_specs=[VMEM_SPEC] * 7,
        out_specs=VMEM_SPEC,
        scratch_shapes=[
            pltpu.VMEM((8, 32, 128), BF),
            pltpu.VMEM((8, 32, 128), BF),
            pltpu.VMEM((8, 32, 128), BF),
            pltpu.VMEM((3, 8, 32, 128), BF),
            pltpu.VMEM((3, 8, SLOTS), F32),
            pltpu.VMEM((3, FZ, SLOTS), BF),
            pltpu.VMEM((2, 2, 256, SLOTS), BF),
            pltpu.VMEM((2, 512, FZ), F32),
            pltpu.VMEM((2, 256, 256), F32),
            pltpu.VMEM((2, 2, CA, 16, 256), BF),
            pltpu.VMEM((2, 2, CA, 16, 256), BF),
            pltpu.VMEM((256, 512), BF),
            pltpu.VMEM((128, 256), BF),
            pltpu.VMEM((CA, NZ), F32),
            pltpu.VMEM((CY, NZ), F32),
            pltpu.SemaphoreType.DMA((7,)),
            pltpu.SemaphoreType.DMA((7,)),
            pltpu.SemaphoreType.DMA((7,)),
            pltpu.SemaphoreType.DMA((7,)),
            pltpu.SemaphoreType.DMA((2,)),
            pltpu.SemaphoreType.DMA((2,)),
            pltpu.SemaphoreType.DMA((4,)),
            pltpu.SemaphoreType.DMA((4,)),
        ],
        compiler_params=pltpu.CompilerParams(vmem_limit_bytes=56 << 20, collective_id=0, has_side_effects=True),
        name="deposit_and_smooth",
    )(parcels[0, 0], cell_index[0, 0], counts[0], coupling, jnp.asarray(_kx()), jnp.asarray(_ky()), jnp.asarray(_kz()))


def solution(mesh):
    return jax.shard_map(
        on_device,
        mesh=mesh,
        in_specs=(
            P("ax", "cr", None, None, None),
            P("ax", "cr", None, None),
            P("ax", "cr", None),
            P(),
        ),
        out_specs=P(None, "ax", "cr", None),
        check_vma=False,
    )
```

```python
import math

import jax
import jax.numpy as jnp
import ml_dtypes
import numpy as np
from jax import lax
from jax.experimental import pallas as pl
from jax.experimental.pallas import tpu as pltpu
from jax.sharding import PartitionSpec as P

CA = 32
CY = 32
NZ = 128
COMP = 4
HALF = 16
NX = 384
NY = 2048
SLOTS = 4096
FZ = COMP * NZ
BF = jnp.bfloat16
F32 = jnp.float32
NT = (((1,), (1,)), ((), ()))

VOLUME = 256.0
SIGMA = 0.75 * HALF
TAPS = [math.exp(-k * k / (2.0 * SIGMA * SIGMA)) for k in range(HALF + 1)]
STRETCH = 1.8433
HELD = [float(np.float32(STRETCH * t).astype(ml_dtypes.bfloat16)) for t in TAPS]
_W = [1.0] + [2.0] * HALF
UNDO = sum(w * h * t for w, h, t in zip(_W, HELD, TAPS)) / sum(w * h * h for w, h in zip(_W, HELD))


ROWS = 16


def iota(shape, axis):
    return lax.broadcasted_iota(jnp.int32, shape, axis)


def weight_sum(pos, extent):
    total = jnp.zeros(pos.shape, F32)
    for k in range(-HALF, HALF + 1):
        inside = (pos + k >= 0) & (pos + k < extent)
        total = total + jnp.where(inside, TAPS[abs(k)], 0.0)
    return total


def taps_at(gap, where):
    value = jnp.zeros(gap.shape, F32)
    for k in range(HALF + 1):
        value = jnp.where(gap == k, HELD[k], value)
    return jnp.where(where, value, 0.0).astype(BF)


def axial_band(below, above):
    r, s = iota((256, 512), 0), iota((256, 512), 1)
    own, low = s < 256, s < 384
    row = jnp.where(own, s >> 5, (s >> 4) & 7)
    layer = jnp.where(own, s & 31, jnp.where(low, (s & 15) - 16, (s & 15) + 32))
    there = own | (jnp.where(low, below, above) > 0)
    return taps_at(jnp.abs((r >> 3) - layer), ((r & 7) == row) & there)


def cross_band(below, above):
    r, s = iota((128, 256), 0), iota((128, 256), 1)
    part = s >> 6
    row = (s & 15) + jnp.where(part < 2, part * 16, jnp.where(part == 2, -16, 32))
    there = (part < 2) | (jnp.where(part == 2, below, above) > 0)
    return taps_at(jnp.abs((r & 31) - row), ((r >> 5) == ((s >> 4) & 3)) & there)


def depth_band():
    r, s = iota((256, NZ), 0), iota((256, NZ), 1)
    return taps_at(jnp.abs((r & 127) - s), s >= 0)


def split(v):
    high = v.astype(BF)
    return high, (v - high.astype(F32)).astype(BF)


def whole_kernel(
    parcels_hbm, cell_hbm, counts_hbm, coupling_hbm, out_ref,
    parcels_ref, cell_ref, counts_ref, coupling_ref, msg1, buf1, msg2, lists, flat, wt, picks, acc_own, acc_side, e_own, e_side, kxs, kys, kzs, sx, syz, load,
    send1, recv1, send2, recv2, send_ax, recv_ax, send_cr, recv_cr,
):
    a, c_at = lax.axis_index("ax"), lax.axis_index("cr")
    n_ax, n_cr = lax.axis_size("ax"), lax.axis_size("cr")
    y_at, g_at = c_at // 8, c_at % 8
    up, down = lax.rem(a + 1, n_ax), lax.rem(a + n_ax - 1, n_ax)
    right, left = lax.rem(c_at + 1, n_cr), lax.rem(c_at + n_cr - 1, n_cr)
    in_row = [(a, y_at * 8 + lax.rem(g_at + j, 8)) for j in range(1, 8)]
    in_column = [(a, lax.rem(y_at + j, 8) * 8 + g_at) for j in range(1, 8)]

    def remote(src, dst, send, recv, to):
        return pltpu.make_async_remote_copy(
            src_ref=src, dst_ref=dst, send_sem=send, recv_sem=recv, device_id=to, device_id_type=pl.DeviceIdType.MESH
        )

    loads = [
        pltpu.make_async_copy(src, dst, load.at[k])
        for k, (src, dst) in enumerate(
            [(parcels_hbm, parcels_ref), (cell_hbm, cell_ref), (counts_hbm, counts_ref), (coupling_hbm, coupling_ref)]
        )
    ]
    for copy in loads:
        copy.start()
    barrier = pltpu.get_barrier_semaphore()
    partners = in_row + in_column + [(up, c_at), (down, c_at), (a, right), (a, left)]
    for to in partners:
        pl.semaphore_signal(barrier, inc=1, device_id=to, device_id_type=pl.DeviceIdType.MESH)

    one, zero = jnp.ones((), BF), jnp.zeros((), BF)
    for copy in loads:
        copy.wait()

    r, s = iota((128, 4), 0), iota((128, 4), 1)
    spread = jnp.dot(((r & 7) == s).astype(F32).astype(BF), coupling_ref[...], preferred_element_type=F32).astype(BF)
    r, s = iota((16, 256), 0), iota((16, 256), 1)
    spread = jnp.dot(spread, ((s & 15) == r).astype(F32).astype(BF), preferred_element_type=F32)
    r, s = iota((128, 256), 0), iota((128, 256), 1)
    mix = jnp.where((r >> 3) == (s >> 4), spread, 0.0).astype(BF)
    eye = (iota((64, 64), 0) == iota((64, 64), 1)).astype(F32).astype(BF)
    counts = jnp.broadcast_to(counts_ref[...].astype(F32), (64, 64)).astype(BF)
    counts = lax.dot_general(eye, counts, NT, preferred_element_type=F32)
    live = iota((64, 64), 1).astype(F32) < counts
    cell = cell_ref[...]
    codes = []
    for code in (jnp.where(live, cell & 127, -1), (cell >> 7) & 31, cell >> 12):
        code = code.astype(F32)
        codes.append(jnp.concatenate([code[:32], code[32:]], axis=1))
    codes = jnp.concatenate(codes, axis=0).astype(BF)
    for group in range(2):
        records = []
        for b in range(16):
            d = (b % 4) * 8 + 4 * group + b // 4
            records.append(jnp.concatenate([parcels_ref[d], parcels_ref[d + 32]], axis=1))
        letter = jnp.dot(mix, jnp.concatenate(records, axis=0), preferred_element_type=F32)
        r, s = iota((128, 96), 0), iota((128, 96), 1)
        b = r >> 3
        choose = ((r & 7) == 4 + (s >> 5)) & ((s & 31) == (b & 3) * 8 + 4 * group + (b >> 2))
        letter += jnp.dot(choose.astype(F32).astype(BF), codes, preferred_element_type=F32)
        msg1[group * 4 : group * 4 + 4] = letter.astype(BF).reshape(4, 32, 128)

    pl.semaphore_wait(barrier, len(partners))
    first = []
    for j in range(1, 8):
        first.append(remote(msg1.at[lax.rem(g_at + j, 8)], buf1.at[g_at], send1.at[j - 1], recv1.at[j - 1], in_row[j - 1]))
        first[-1].start()
    buf1[g_at] = msg1[g_at]

    kxs[...] = axial_band(a, n_ax - 1 - a)
    kys[...] = cross_band(c_at, n_cr - 1 - c_at)
    kzs[...] = depth_band()
    sx[...] = 1.0 / weight_sum(iota((CA, NZ), 0) + a * CA, NX)
    syz[...] = (VOLUME * UNDO**3) / (
        weight_sum(iota((CY, NZ), 0) + c_at * CY, NY) * weight_sum(iota((8, NZ), 1), NZ)[0:1, :]
    )

    for copy in first:
        copy.wait_recv()
    near = iota((32, 128), 1) < 64
    halves = []
    for m in range(4):
        p, q = buf1[2 * m].astype(F32), buf1[2 * m + 1].astype(F32)
        halves.append((jnp.where(near, p, pltpu.roll(q, 64, 1)), jnp.where(near, pltpu.roll(p, 64, 1), q)))
    for h in range(2):
        for i in range(4):
            msg2[4 * h + i] = jnp.concatenate([halves[m][h][i * 8 : i * 8 + 8] for m in range(4)], axis=0).astype(BF)
    second = []
    for j in range(1, 8):
        second.append(
            remote(
                msg2.at[lax.rem(y_at + j, 8)], lists.at[0, y_at], send2.at[j - 1], recv2.at[j - 1], in_column[j - 1]
            )
        )
        second[-1].start()
    lists[0, y_at] = msg2[y_at]
    for copy in second:
        copy.wait_recv()
    along = [
        remote(lists.at[0], lists.at[1], send_ax.at[0], recv_ax.at[0], (up, c_at)),
        remote(lists.at[0], lists.at[2], send_ax.at[1], recv_ax.at[1], (down, c_at)),
    ]
    for copy in along:
        copy.start()

    def rows_iota(n, width):
        return iota((n, width), 0).astype(F32).astype(BF)

    def unfold(l):
        rows = lists[l].astype(F32).reshape(256, 128)
        flat[l] = jnp.concatenate([rows[b * 8 : b * 8 + 8] for b in range(32)], axis=1)
        width = 1024
        for b in range(SLOTS // width):
            ks = pl.ds(b * width, width)
            hit = jnp.broadcast_to(flat[l, 4:5, ks].astype(BF), (NZ, width)) == rows_iota(NZ, width)
            for f in range(COMP):
                source = jnp.broadcast_to(flat[l, f : f + 1, ks].astype(BF), (NZ, width))
                wt[l, f * NZ : (f + 1) * NZ, ks] = jnp.where(hit, source, zero)

    def picked(l, c):
        n, x0 = (32, 0) if l == 0 else (16, 16 if l == 1 else 0)
        y = flat[l, 5:6, :] - float(c * ROWS)
        x = flat[l, 6:7, :] - float(x0)
        ok = (x >= 0) & (x < n)
        parts = []
        for i in range(ROWS):
            key = jnp.where(ok & (y == i), x, -1.0).astype(BF)
            parts.append(jnp.where(jnp.broadcast_to(key, (n, SLOTS)) == rows_iota(n, SLOTS), one, zero))
        return jnp.concatenate(parts, axis=0)

    unfold(0)
    for c in range(2):
        acc_own[c] = lax.dot_general(picked(0, c), wt[0], NT, preferred_element_type=F32)
    for l in (1, 2):
        along[l - 1].wait_recv()
        unfold(l)
    across = []
    for h in range(2):
        fs = slice(h * 256, h * 256 + 256)
        for c in range(2):
            for l in (1, 2):
                if h == 0:
                    picks[c, l - 1] = picked(l, c)
                acc_side[l - 1] = lax.dot_general(picks[c, l - 1], wt[l, fs, :], NT, preferred_element_type=F32)
            done = []
            for i in range(2):
                own = acc_own[c, i * 256 : i * 256 + 256, fs]
                sides = [acc_side[k, i * 128 : i * 128 + 128, :] for k in range(2)]
                high, low = split(jnp.concatenate([own] + sides, axis=0))
                v = jnp.dot(kxs[...], high, preferred_element_type=F32)
                v += jnp.dot(kxs[...], low, preferred_element_type=F32)
                done.append(v.reshape(CA, 8, 256))
            e_own[h, c] = jnp.concatenate(done, axis=1).astype(BF)
            k = h * 2 + c
            across.append(remote(e_own.at[h, c], e_side.at[h, 1 - c], send_cr.at[k], recv_cr.at[k], (a, (left, right)[c])))
            across[-1].start()
    for h in range(2):
        across[2 * h].wait_recv()
        across[2 * h + 1].wait_recv()

        for g in range(CA // 4):
            xs = slice(g * 4, g * 4 + 4)
            rhs = [e_own[h, c, xs].reshape(64, 256) for c in range(2)] + [e_side[h, c, xs].reshape(64, 256) for c in range(2)]
            v = jnp.dot(kys[...], jnp.concatenate(rhs, axis=0), preferred_element_type=F32)
            high, low = split(jnp.concatenate([v[:, :128], v[:, 128:]], axis=0))
            v = jnp.dot(jnp.concatenate([high, low], axis=1), kzs[...], preferred_element_type=F32)
            v = v.reshape(2, 4, CY, NZ)
            for i in range(4):
                scale = syz[...] * sx[g * 4 + i : g * 4 + i + 1, :]
                for f in range(2):
                    out_ref[2 * h + f, g * 4 + i] = v[f, i] * scale
    for copy in first + second + along + across:
        copy.wait_send()


VMEM_SPEC = pl.BlockSpec(memory_space=pltpu.VMEM)


def on_device(parcels, cell_index, counts, coupling):
    return pl.pallas_call(
        whole_kernel,
        out_shape=jax.ShapeDtypeStruct((COMP, CA, CY, NZ), F32),
        in_specs=[pl.BlockSpec(memory_space=pltpu.HBM)] * 4,
        out_specs=VMEM_SPEC,
        scratch_shapes=[
            pltpu.VMEM((64, 16, 64), BF),
            pltpu.VMEM((64, 64), jnp.int32),
            pltpu.VMEM((1, 64), jnp.int32),
            pltpu.VMEM((COMP, 16), BF),
            pltpu.VMEM((8, 32, 128), BF),
            pltpu.VMEM((8, 32, 128), BF),
            pltpu.VMEM((8, 32, 128), BF),
            pltpu.VMEM((3, 8, 32, 128), BF),
            pltpu.VMEM((3, 8, SLOTS), F32),
            pltpu.VMEM((3, FZ, SLOTS), BF),
            pltpu.VMEM((2, 2, 256, SLOTS), BF),
            pltpu.VMEM((2, 512, FZ), F32),
            pltpu.VMEM((2, 256, 256), F32),
            pltpu.VMEM((2, 2, CA, 16, 256), BF),
            pltpu.VMEM((2, 2, CA, 16, 256), BF),
            pltpu.VMEM((256, 512), BF),
            pltpu.VMEM((128, 256), BF),
            pltpu.VMEM((256, NZ), BF),
            pltpu.VMEM((CA, NZ), F32),
            pltpu.VMEM((CY, NZ), F32),
            pltpu.SemaphoreType.DMA((4,)),
            pltpu.SemaphoreType.DMA((7,)),
            pltpu.SemaphoreType.DMA((7,)),
            pltpu.SemaphoreType.DMA((7,)),
            pltpu.SemaphoreType.DMA((7,)),
            pltpu.SemaphoreType.DMA((2,)),
            pltpu.SemaphoreType.DMA((2,)),
            pltpu.SemaphoreType.DMA((4,)),
            pltpu.SemaphoreType.DMA((4,)),
        ],
        compiler_params=pltpu.CompilerParams(vmem_limit_bytes=40 << 20, collective_id=0, has_side_effects=True),
        name="deposit_and_smooth",
    )(parcels[0, 0], cell_index[0, 0], counts[0], coupling)


def solution(mesh):
    return jax.shard_map(
        on_device,
        mesh=mesh,
        in_specs=(
            P("ax", "cr", None, None, None),
            P("ax", "cr", None, None),
            P("ax", "cr", None),
            P(),
        ),
        out_specs=P(None, "ax", "cr", None),
        check_vma=False,
    )
```

```python
import math

import jax
import jax.numpy as jnp
import ml_dtypes
import numpy as np
from jax import lax
from jax.experimental import pallas as pl
from jax.experimental.pallas import tpu as pltpu
from jax.sharding import PartitionSpec as P

CA = 32
CY = 32
NZ = 128
COMP = 4
HALF = 16
NX = 384
NY = 2048
SLOTS = 4096
FZ = COMP * NZ
BF = jnp.bfloat16
F32 = jnp.float32
NT = (((1,), (1,)), ((), ()))

VOLUME = 256.0
SIGMA = 0.75 * HALF
TAPS = [math.exp(-k * k / (2.0 * SIGMA * SIGMA)) for k in range(HALF + 1)]
STRETCH = 1.8433
HELD = [float(np.float32(STRETCH * t).astype(ml_dtypes.bfloat16)) for t in TAPS]
_W = [1.0] + [2.0] * HALF
UNDO = sum(w * h * t for w, h, t in zip(_W, HELD, TAPS)) / sum(w * h * h for w, h in zip(_W, HELD))


ROWS = 16


def iota(shape, axis):
    return lax.broadcasted_iota(jnp.int32, shape, axis)


def weight_sum(pos, extent):
    total = jnp.zeros(pos.shape, F32)
    for k in range(-HALF, HALF + 1):
        inside = (pos + k >= 0) & (pos + k < extent)
        total = total + jnp.where(inside, TAPS[abs(k)], 0.0)
    return total


def taps_at(gap, where):
    value = jnp.zeros(gap.shape, F32)
    for k in range(HALF + 1):
        value = jnp.where(gap == k, HELD[k], value)
    return jnp.where(where, value, 0.0).astype(BF)


def axial_band(below, above):
    r, s = iota((256, 512), 0), iota((256, 512), 1)
    own, low = s < 256, s < 384
    row = jnp.where(own, s >> 5, (s >> 4) & 7)
    layer = jnp.where(own, s & 31, jnp.where(low, (s & 15) - 16, (s & 15) + 32))
    there = own | (jnp.where(low, below, above) > 0)
    return taps_at(jnp.abs((r >> 3) - layer), ((r & 7) == row) & there)


def cross_band(below, above):
    r, s = iota((128, 256), 0), iota((128, 256), 1)
    part = s >> 5
    row = (s & 7) + part * 8 - jnp.where(part < 4, 0, jnp.where(part < 6, 48, 16))
    there = (part < 4) | (jnp.where(part < 6, below, above) > 0)
    return taps_at(jnp.abs((r & 31) - row), ((r >> 5) == ((s >> 3) & 3)) & there)


def depth_band():
    r, s = iota((256, NZ), 0), iota((256, NZ), 1)
    return taps_at(jnp.abs((r & 127) - s), s >= 0)


def split(v):
    high = v.astype(BF)
    return high, (v - high.astype(F32)).astype(BF)


def whole_kernel(
    parcels_hbm, cell_hbm, counts_hbm, coupling_hbm, out_ref,
    parcels_ref, cell_ref, counts_ref, coupling_ref, msg1, buf1, msg2, lists, flat, keys, wt, picks, acc_own, acc_side, e_own, e_side, kxs, kys, kzs, sx, syz, load,
    send1, recv1, send2, recv2, send_ax, recv_ax, send_cr, recv_cr,
):
    a, c_at = lax.axis_index("ax"), lax.axis_index("cr")
    n_ax, n_cr = lax.axis_size("ax"), lax.axis_size("cr")
    y_at, g_at = c_at // 8, c_at % 8
    up, down = lax.rem(a + 1, n_ax), lax.rem(a + n_ax - 1, n_ax)
    right, left = lax.rem(c_at + 1, n_cr), lax.rem(c_at + n_cr - 1, n_cr)
    in_row = [(a, y_at * 8 + lax.rem(g_at + j, 8)) for j in range(1, 8)]
    in_column = [(a, lax.rem(y_at + j, 8) * 8 + g_at) for j in range(1, 8)]

    def remote(src, dst, send, recv, to):
        return pltpu.make_async_remote_copy(
            src_ref=src, dst_ref=dst, send_sem=send, recv_sem=recv, device_id=to, device_id_type=pl.DeviceIdType.MESH
        )

    loads = [
        pltpu.make_async_copy(src, dst, load.at[k])
        for k, (src, dst) in enumerate(
            [(parcels_hbm, parcels_ref), (cell_hbm, cell_ref), (counts_hbm, counts_ref), (coupling_hbm, coupling_ref)]
        )
    ]
    for copy in loads:
        copy.start()
    barrier = pltpu.get_barrier_semaphore()
    partners = in_row + in_column + [(up, c_at), (down, c_at), (a, right), (a, left)]
    for to in partners:
        pl.semaphore_signal(barrier, inc=1, device_id=to, device_id_type=pl.DeviceIdType.MESH)

    one, zero = jnp.ones((), BF), jnp.zeros((), BF)
    for copy in loads:
        copy.wait()

    r, s = iota((128, 4), 0), iota((128, 4), 1)
    spread = jnp.dot(((r & 7) == s).astype(F32).astype(BF), coupling_ref[...], preferred_element_type=F32).astype(BF)
    r, s = iota((16, 256), 0), iota((16, 256), 1)
    spread = jnp.dot(spread, ((s & 15) == r).astype(F32).astype(BF), preferred_element_type=F32)
    r, s = iota((128, 256), 0), iota((128, 256), 1)
    mix = jnp.where((r >> 3) == (s >> 4), spread, 0.0).astype(BF)
    eye = (iota((64, 64), 0) == iota((64, 64), 1)).astype(F32).astype(BF)
    counts = jnp.broadcast_to(counts_ref[...].astype(F32), (64, 64)).astype(BF)
    counts = lax.dot_general(eye, counts, NT, preferred_element_type=F32)
    live = iota((64, 64), 1).astype(F32) < counts
    cell = cell_ref[...]
    codes = []
    for code in (jnp.where(live, cell & 127, -1), (cell >> 7) & 31, cell >> 12):
        code = code.astype(F32)
        codes.append(jnp.concatenate([code[:32], code[32:]], axis=1))
    codes = jnp.concatenate(codes, axis=0).astype(BF)
    for group in range(2):
        records = []
        for b in range(16):
            d = (b % 4) * 8 + 4 * group + b // 4
            records.append(jnp.concatenate([parcels_ref[d], parcels_ref[d + 32]], axis=1))
        letter = jnp.dot(mix, jnp.concatenate(records, axis=0), preferred_element_type=F32)
        r, s = iota((128, 96), 0), iota((128, 96), 1)
        b = r >> 3
        choose = ((r & 7) == 4 + (s >> 5)) & ((s & 31) == (b & 3) * 8 + 4 * group + (b >> 2))
        letter += jnp.dot(choose.astype(F32).astype(BF), codes, preferred_element_type=F32)
        msg1[group * 4 : group * 4 + 4] = letter.astype(BF).reshape(4, 32, 128)

    pl.semaphore_wait(barrier, len(partners))
    first = []
    for j in range(1, 8):
        first.append(remote(msg1.at[lax.rem(g_at + j, 8)], buf1.at[g_at], send1.at[j - 1], recv1.at[j - 1], in_row[j - 1]))
        first[-1].start()
    buf1[g_at] = msg1[g_at]

    kxs[...] = axial_band(a, n_ax - 1 - a)
    kys[...] = cross_band(c_at, n_cr - 1 - c_at)
    kzs[...] = depth_band()
    sx[...] = 1.0 / weight_sum(iota((CA, NZ), 0) + a * CA, NX)
    syz[...] = (VOLUME * UNDO**3) / (
        weight_sum(iota((CY, NZ), 0) + c_at * CY, NY) * weight_sum(iota((8, NZ), 1), NZ)[0:1, :]
    )

    for copy in first:
        copy.wait_recv()
    near = iota((32, 128), 1) < 64
    halves = []
    for m in range(4):
        p, q = buf1[2 * m].astype(F32), buf1[2 * m + 1].astype(F32)
        halves.append((jnp.where(near, p, pltpu.roll(q, 64, 1)), jnp.where(near, pltpu.roll(p, 64, 1), q)))
    for h in range(2):
        for i in range(4):
            msg2[4 * h + i] = jnp.concatenate([halves[m][h][i * 8 : i * 8 + 8] for m in range(4)], axis=0).astype(BF)
    second = {}
    for j in (4, 3, 5, 2, 6, 1, 7):
        second[j] = remote(
            msg2.at[lax.rem(y_at + j, 8)], lists.at[0, y_at], send2.at[j - 1], recv2.at[j - 1], in_column[j - 1]
        )
        second[j].start()
    lists[0, y_at] = msg2[y_at]

    def rows_iota(n, width):
        return iota((n, width), 0).astype(F32).astype(BF)

    def source(j):
        return lax.rem(y_at + 8 - j, 8)

    def unfold(l, j, ks):
        rows = lists[l, source(j)].astype(F32)
        flat[l, :, ks] = jnp.concatenate([rows[b * 8 : b * 8 + 8] for b in range(4)], axis=1)
        hit = jnp.broadcast_to(flat[l, 4:5, ks].astype(BF), (NZ, 512)) == rows_iota(NZ, 512)
        for f in range(COMP):
            term = jnp.broadcast_to(flat[l, f : f + 1, ks].astype(BF), (NZ, 512))
            wt[l, f * NZ : (f + 1) * NZ, ks] = jnp.where(hit, term, zero)
        n, x0 = (32, 0) if l == 0 else (16, 16 if l == 1 else 0)
        y = jnp.broadcast_to(flat[l, 5:6, ks], (CY, 512))
        x = jnp.broadcast_to(flat[l, 6:7, ks], (CY, 512)) - float(x0)
        here = (y == iota((CY, 512), 0).astype(F32)) & (x >= 0) & (x < n)
        keys[l, :, ks] = jnp.where(here, x, -1.0)

    def picked(l, rows, ks, width):
        n = 32 if l == 0 else 16
        parts = []
        for i in rows:
            key = jnp.broadcast_to(keys[l, i : i + 1, ks].astype(BF), (n, width))
            parts.append(jnp.where(key == rows_iota(n, width), one, zero))
        return jnp.concatenate(parts, axis=0)

    along = {}
    at = 0
    order = ((0,), (1, 7), (2, 6), (3, 5), (4,))
    for step in order:
        for j in step:
            if j:
                second[j].wait_recv()
            for k, to in ((0, up), (1, down)):
                along[k, j] = remote(
                    lists.at[0, source(j)], lists.at[1 + k, source(j)], send_ax.at[k, j], recv_ax.at[k, j], (to, c_at)
                )
                along[k, j].start()
        for b, j in enumerate(step):
            unfold(0, j, slice(at + b * 512, at + b * 512 + 512))
        width = 512 * len(step)
        ks = slice(at, at + width)
        for c in range(2):
            d = lax.dot_general(
                picked(0, range(c * ROWS, c * ROWS + ROWS), ks, width), wt[0, :, ks], NT, preferred_element_type=F32
            )
            acc_own[c] = d if at == 0 else acc_own[c] + d
        at += width
    at = 0
    for step in order:
        for j in step:
            for l in (1, 2):
                along[l - 1, j].wait_recv()
                unfold(l, j, slice(at, at + 512))
            at += 512
    across = []
    for h in range(2):
        fs = slice(h * 256, h * 256 + 256)
        for i in range(2):
            for l in (1, 2):
                if h == 0:
                    rows = [c * ROWS + i * 8 + k for c in range(2) for k in range(8)]
                    picks[i, l - 1] = picked(l, rows, slice(0, SLOTS), SLOTS)
                acc_side[l - 1] = lax.dot_general(picks[i, l - 1], wt[l, fs, :], NT, preferred_element_type=F32)
            for c in range(2):
                own = acc_own[c, i * 256 : i * 256 + 256, fs]
                sides = [acc_side[k, c * 128 : c * 128 + 128, :] for k in range(2)]
                high, low = split(jnp.concatenate([own] + sides, axis=0))
                v = jnp.dot(kxs[...], high, preferred_element_type=F32)
                v += jnp.dot(kxs[...], low, preferred_element_type=F32)
                e_own[h, i, c] = v.astype(BF).reshape(16, 16, 256)
                k = h * 4 + i * 2 + c
                across.append(
                    remote(e_own.at[h, i, c], e_side.at[h, i, 1 - c], send_cr.at[k], recv_cr.at[k], (a, (left, right)[c]))
                )
                across[-1].start()
    for h in range(2):
        for copy in across[4 * h : 4 * h + 4]:
            copy.wait_recv()
        for g in range(CA // 4):
            xs = slice(g * 2, g * 2 + 2)
            rhs = [e[h, i, c, xs].reshape(32, 256) for e in (e_own, e_side) for c in range(2) for i in range(2)]
            v = jnp.dot(kys[...], jnp.concatenate(rhs, axis=0), preferred_element_type=F32)
            high, low = split(jnp.concatenate([v[:, :128], v[:, 128:]], axis=0))
            v = jnp.dot(jnp.concatenate([high, low], axis=1), kzs[...], preferred_element_type=F32)
            v = v.reshape(2, 4, CY, NZ)
            for i in range(4):
                scale = syz[...] * sx[g * 4 + i : g * 4 + i + 1, :]
                for f in range(2):
                    out_ref[2 * h + f, g * 4 + i] = v[f, i] * scale
    for copy in first + list(second.values()) + list(along.values()) + across:
        copy.wait_send()


VMEM_SPEC = pl.BlockSpec(memory_space=pltpu.VMEM)


def on_device(parcels, cell_index, counts, coupling):
    inputs = [pltpu.with_memory_space_constraint(v, pltpu.HBM) for v in (parcels[0, 0], cell_index[0, 0], counts[0], coupling)]
    return pl.pallas_call(
        whole_kernel,
        out_shape=jax.ShapeDtypeStruct((COMP, CA, CY, NZ), F32),
        in_specs=[pl.BlockSpec(memory_space=pltpu.HBM)] * 4,
        out_specs=VMEM_SPEC,
        scratch_shapes=[
            pltpu.VMEM((64, 16, 64), BF),
            pltpu.VMEM((64, 64), jnp.int32),
            pltpu.VMEM((1, 64), jnp.int32),
            pltpu.VMEM((COMP, 16), BF),
            pltpu.VMEM((8, 32, 128), BF),
            pltpu.VMEM((8, 32, 128), BF),
            pltpu.VMEM((8, 32, 128), BF),
            pltpu.VMEM((3, 8, 32, 128), BF),
            pltpu.VMEM((3, 8, SLOTS), F32),
            pltpu.VMEM((3, CY, SLOTS), F32),
            pltpu.VMEM((3, FZ, SLOTS), BF),
            pltpu.VMEM((2, 2, 256, SLOTS), BF),
            pltpu.VMEM((2, 512, FZ), F32),
            pltpu.VMEM((2, 256, 256), F32),
            pltpu.VMEM((2, 2, 2, 16, 16, 256), BF),
            pltpu.VMEM((2, 2, 2, 16, 16, 256), BF),
            pltpu.VMEM((256, 512), BF),
            pltpu.VMEM((128, 256), BF),
            pltpu.VMEM((256, NZ), BF),
            pltpu.VMEM((CA, NZ), F32),
            pltpu.VMEM((CY, NZ), F32),
            pltpu.SemaphoreType.DMA((4,)),
            pltpu.SemaphoreType.DMA((7,)),
            pltpu.SemaphoreType.DMA((7,)),
            pltpu.SemaphoreType.DMA((7,)),
            pltpu.SemaphoreType.DMA((7,)),
            pltpu.SemaphoreType.DMA((2, 8)),
            pltpu.SemaphoreType.DMA((2, 8)),
            pltpu.SemaphoreType.DMA((8,)),
            pltpu.SemaphoreType.DMA((8,)),
        ],
        compiler_params=pltpu.CompilerParams(vmem_limit_bytes=40 << 20, collective_id=0, has_side_effects=True),
        name="deposit_and_smooth",
    )(*inputs)


def solution(mesh):
    return jax.shard_map(
        on_device,
        mesh=mesh,
        in_specs=(
            P("ax", "cr", None, None, None),
            P("ax", "cr", None, None),
            P("ax", "cr", None),
            P(),
        ),
        out_specs=P(None, "ax", "cr", None),
        check_vma=False,
    )
```

```python
import math

import jax
import jax.numpy as jnp
import ml_dtypes
import numpy as np
from jax import lax
from jax.experimental import pallas as pl
from jax.experimental.pallas import tpu as pltpu
from jax.sharding import PartitionSpec as P

CA = 32
CY = 32
NZ = 128
COMP = 4
HALF = 16
NX = 384
NY = 2048
SLOTS = 4096
FZ = COMP * NZ
BF = jnp.bfloat16
F32 = jnp.float32
NT = (((1,), (1,)), ((), ()))

VOLUME = 256.0
SIGMA = 0.75 * HALF
TAPS = [math.exp(-k * k / (2.0 * SIGMA * SIGMA)) for k in range(HALF + 1)]
STRETCH = 1.8433
HELD = [float(np.float32(STRETCH * t).astype(ml_dtypes.bfloat16)) for t in TAPS]
_W = [1.0] + [2.0] * HALF
UNDO = sum(w * h * t for w, h, t in zip(_W, HELD, TAPS)) / sum(w * h * h for w, h in zip(_W, HELD))


ROWS = 16


def iota(shape, axis):
    return lax.broadcasted_iota(jnp.int32, shape, axis)


def weight_sum(pos, extent):
    total = jnp.zeros(pos.shape, F32)
    for k in range(-HALF, HALF + 1):
        inside = (pos + k >= 0) & (pos + k < extent)
        total = total + jnp.where(inside, TAPS[abs(k)], 0.0)
    return total


def taps_at(gap, where):
    value = jnp.zeros(gap.shape, F32)
    for k in range(HALF + 1):
        value = jnp.where(gap == k, HELD[k], value)
    return jnp.where(where, value, 0.0).astype(BF)


def axial_band(below, above):
    r, s = iota((256, 512), 0), iota((256, 512), 1)
    own, low = s < 256, s < 384
    row = jnp.where(own, s >> 5, (s >> 4) & 7)
    layer = jnp.where(own, s & 31, jnp.where(low, (s & 15) - 16, (s & 15) + 32))
    there = own | (jnp.where(low, below, above) > 0)
    return taps_at(jnp.abs((r >> 3) - layer), ((r & 7) == row) & there)


def cross_band(below, above):
    r, s = iota((128, 256), 0), iota((128, 256), 1)
    part = s >> 5
    row = (s & 7) + part * 8 - jnp.where(part < 4, 0, jnp.where(part < 6, 48, 16))
    there = (part < 4) | (jnp.where(part < 6, below, above) > 0)
    return taps_at(jnp.abs((r & 31) - row), ((r >> 5) == ((s >> 3) & 3)) & there)


def depth_band():
    r, s = iota((256, NZ), 0), iota((256, NZ), 1)
    return taps_at(jnp.abs((r & 127) - s), s >= 0)


def split(v):
    high = v.astype(BF)
    return high, (v - high.astype(F32)).astype(BF)


def whole_kernel(
    parcels_hbm, cell_hbm, counts_hbm, coupling_hbm, out_ref,
    parcels_ref, cell_ref, counts_ref, coupling_ref, msg1, buf1, msg2, lists, flat, keys, wt, picks, acc_own, axial, acc_side, e_own, e_side, kxs, kys, kzs, sx, syz, load,
    send1, recv1, send2, recv2, send_ax, recv_ax, send_cr, recv_cr,
):
    a, c_at = lax.axis_index("ax"), lax.axis_index("cr")
    n_ax, n_cr = lax.axis_size("ax"), lax.axis_size("cr")
    y_at, g_at = c_at // 8, c_at % 8
    up, down = lax.rem(a + 1, n_ax), lax.rem(a + n_ax - 1, n_ax)
    right, left = lax.rem(c_at + 1, n_cr), lax.rem(c_at + n_cr - 1, n_cr)
    in_row = [(a, y_at * 8 + lax.rem(g_at + j, 8)) for j in range(1, 8)]
    in_column = [(a, lax.rem(y_at + j, 8) * 8 + g_at) for j in range(1, 8)]

    def remote(src, dst, send, recv, to):
        return pltpu.make_async_remote_copy(
            src_ref=src, dst_ref=dst, send_sem=send, recv_sem=recv, device_id=to, device_id_type=pl.DeviceIdType.MESH
        )

    loads = [
        pltpu.make_async_copy(src, dst, load.at[k])
        for k, (src, dst) in enumerate(
            [(parcels_hbm, parcels_ref), (cell_hbm, cell_ref), (counts_hbm, counts_ref), (coupling_hbm, coupling_ref)]
        )
    ]
    for copy in loads:
        copy.start()
    barrier = pltpu.get_barrier_semaphore()
    partners = in_row + in_column + [(up, c_at), (down, c_at), (a, right), (a, left)]
    for to in partners:
        pl.semaphore_signal(barrier, inc=1, device_id=to, device_id_type=pl.DeviceIdType.MESH)

    one, zero = jnp.ones((), BF), jnp.zeros((), BF)
    for copy in loads:
        copy.wait()

    r, s = iota((128, 4), 0), iota((128, 4), 1)
    spread = jnp.dot(((r & 7) == s).astype(F32).astype(BF), coupling_ref[...], preferred_element_type=F32).astype(BF)
    r, s = iota((16, 256), 0), iota((16, 256), 1)
    spread = jnp.dot(spread, ((s & 15) == r).astype(F32).astype(BF), preferred_element_type=F32)
    r, s = iota((128, 256), 0), iota((128, 256), 1)
    mix = jnp.where((r >> 3) == (s >> 4), spread, 0.0).astype(BF)
    eye = (iota((64, 64), 0) == iota((64, 64), 1)).astype(F32).astype(BF)
    counts = jnp.broadcast_to(counts_ref[...].astype(F32), (64, 64)).astype(BF)
    counts = lax.dot_general(eye, counts, NT, preferred_element_type=F32)
    live = iota((64, 64), 1).astype(F32) < counts
    cell = cell_ref[...]
    codes = []
    for code in (jnp.where(live, cell & 127, -1), (cell >> 7) & 31, cell >> 12):
        code = code.astype(F32)
        codes.append(jnp.concatenate([code[:32], code[32:]], axis=1))
    codes = jnp.concatenate(codes, axis=0).astype(BF)
    for group in range(2):
        records = []
        for b in range(16):
            d = (b % 4) * 8 + 4 * group + b // 4
            records.append(jnp.concatenate([parcels_ref[d], parcels_ref[d + 32]], axis=1))
        letter = jnp.dot(mix, jnp.concatenate(records, axis=0), preferred_element_type=F32)
        r, s = iota((128, 96), 0), iota((128, 96), 1)
        b = r >> 3
        choose = ((r & 7) == 4 + (s >> 5)) & ((s & 31) == (b & 3) * 8 + 4 * group + (b >> 2))
        letter += jnp.dot(choose.astype(F32).astype(BF), codes, preferred_element_type=F32)
        msg1[group * 4 : group * 4 + 4] = letter.astype(BF).reshape(4, 32, 128)

    pl.semaphore_wait(barrier, len(partners))
    first = []
    for j in range(1, 8):
        first.append(remote(msg1.at[lax.rem(g_at + j, 8)], buf1.at[g_at], send1.at[j - 1], recv1.at[j - 1], in_row[j - 1]))
        first[-1].start()
    buf1[g_at] = msg1[g_at]

    kxs[...] = axial_band(a, n_ax - 1 - a)
    kys[...] = cross_band(c_at, n_cr - 1 - c_at)
    kzs[...] = depth_band()
    sx[...] = 1.0 / weight_sum(iota((CA, NZ), 0) + a * CA, NX)
    syz[...] = (VOLUME * UNDO**3) / (
        weight_sum(iota((CY, NZ), 0) + c_at * CY, NY) * weight_sum(iota((8, NZ), 1), NZ)[0:1, :]
    )

    for copy in first:
        copy.wait_recv()
    near = iota((32, 128), 1) < 64
    halves = []
    for m in range(4):
        p, q = buf1[2 * m].astype(F32), buf1[2 * m + 1].astype(F32)
        halves.append((jnp.where(near, p, pltpu.roll(q, 64, 1)), jnp.where(near, pltpu.roll(p, 64, 1), q)))
    for h in range(2):
        for i in range(4):
            msg2[4 * h + i] = jnp.concatenate([halves[m][h][i * 8 : i * 8 + 8] for m in range(4)], axis=0).astype(BF)
    place = {j: p for p, j in enumerate((0, 1, 7, 2, 6, 3, 5, 4))}
    second = {}
    for j in (4, 3, 5, 2, 6, 1, 7):
        second[j] = remote(
            msg2.at[lax.rem(y_at + j, 8)], lists.at[0, place[j]], send2.at[j - 1], recv2.at[j - 1], in_column[j - 1]
        )
        second[j].start()
    lists[0, 0] = msg2[y_at]

    def rows_iota(n, width):
        return iota((n, width), 0).astype(F32).astype(BF)

    def unfold(l, p):
        ks = slice(p * 512, p * 512 + 512)
        rows = lists[l, p].astype(F32)
        flat[l, :, ks] = jnp.concatenate([rows[b * 8 : b * 8 + 8] for b in range(4)], axis=1)
        hit = jnp.broadcast_to(flat[l, 4:5, ks].astype(BF), (NZ, 512)) == rows_iota(NZ, 512)
        for f in range(COMP):
            term = jnp.broadcast_to(flat[l, f : f + 1, ks].astype(BF), (NZ, 512))
            wt[l, f * NZ : (f + 1) * NZ, ks] = jnp.where(hit, term, zero)
        n, x0 = (32, 0) if l == 0 else (16, 16 if l == 1 else 0)
        y = jnp.broadcast_to(flat[l, 5:6, ks], (CY, 512))
        x = jnp.broadcast_to(flat[l, 6:7, ks], (CY, 512)) - float(x0)
        here = (y == iota((CY, 512), 0).astype(F32)) & (x >= 0) & (x < n)
        keys[l, :, ks] = jnp.where(here, x, -1.0)

    def picked(l, rows, ks, width):
        n = 32 if l == 0 else 16
        parts = []
        for i in rows:
            key = jnp.broadcast_to(keys[l, i : i + 1, ks].astype(BF), (n, width))
            parts.append(jnp.where(key == rows_iota(n, width), one, zero))
        return jnp.concatenate(parts, axis=0)

    def deposit(first_place, last_place):
        for p in range(first_place, last_place):
            unfold(0, p)
        ks = slice(first_place * 512, last_place * 512)
        for c in range(2):
            rows = range(c * ROWS, c * ROWS + ROWS)
            d = lax.dot_general(
                picked(0, rows, ks, ks.stop - ks.start), wt[0, :, ks], NT, preferred_element_type=F32
            )
            acc_own[c] = d if first_place == 0 else acc_own[c] + d

    along = {}

    def hand_on(part, first_place, last_place):
        ps = pl.ds(first_place, last_place - first_place)
        for k, to in ((0, up), (1, down)):
            along[k, part] = remote(
                lists.at[0, ps], lists.at[1 + k, ps], send_ax.at[k, part], recv_ax.at[k, part], (to, c_at)
            )
            along[k, part].start()

    deposit(0, 1)
    for j in (1, 7):
        second[j].wait_recv()
    hand_on(0, 0, 3)
    deposit(1, 3)
    for j in (2, 6, 3, 5, 4):
        second[j].wait_recv()
    hand_on(1, 3, 8)
    deposit(3, 8)
    for h in range(2):
        for i in range(2):
            for c in range(2):
                high, low = split(acc_own[c, i * 256 : i * 256 + 256, h * 256 : h * 256 + 256])
                v = jnp.dot(kxs[:, :256], high, preferred_element_type=F32)
                v += jnp.dot(kxs[:, :256], low, preferred_element_type=F32)
                axial[h, i, c] = v
    for part, places in enumerate((range(3), range(3, 8))):
        for l in (1, 2):
            along[l - 1, part].wait_recv()
            for p in places:
                unfold(l, p)
    across = []
    for h in range(2):
        fs = slice(h * 256, h * 256 + 256)
        for i in range(2):
            for l in (1, 2):
                if h == 0:
                    rows = [c * ROWS + i * 8 + k for c in range(2) for k in range(8)]
                    picks[i, l - 1] = picked(l, rows, slice(0, SLOTS), SLOTS)
                acc_side[l - 1] = lax.dot_general(picks[i, l - 1], wt[l, fs, :], NT, preferred_element_type=F32)
            for c in range(2):
                sides = [acc_side[k, c * 128 : c * 128 + 128, :] for k in range(2)]
                high, low = split(jnp.concatenate(sides, axis=0))
                v = jnp.dot(kxs[:, 256:], high, preferred_element_type=F32)
                v += jnp.dot(kxs[:, 256:], low, preferred_element_type=F32)
                v += axial[h, i, c]
                e_own[h, i, c] = v.astype(BF).reshape(16, 16, 256)
                k = h * 4 + i * 2 + c
                across.append(
                    remote(e_own.at[h, i, c], e_side.at[h, i, 1 - c], send_cr.at[k], recv_cr.at[k], (a, (left, right)[c]))
                )
                across[-1].start()
    for h in range(2):
        for copy in across[4 * h : 4 * h + 4]:
            copy.wait_recv()
        for g in range(CA // 4):
            xs = slice(g * 2, g * 2 + 2)
            rhs = [e[h, i, c, xs].reshape(32, 256) for e in (e_own, e_side) for c in range(2) for i in range(2)]
            v = jnp.dot(kys[...], jnp.concatenate(rhs, axis=0), preferred_element_type=F32)
            high, low = split(jnp.concatenate([v[:, :128], v[:, 128:]], axis=0))
            v = jnp.dot(jnp.concatenate([high, low], axis=1), kzs[...], preferred_element_type=F32)
            v = v.reshape(2, 4, CY, NZ)
            for i in range(4):
                scale = syz[...] * sx[g * 4 + i : g * 4 + i + 1, :]
                for f in range(2):
                    out_ref[2 * h + f, g * 4 + i] = v[f, i] * scale
    for copy in first + list(second.values()) + list(along.values()) + across:
        copy.wait_send()


VMEM_SPEC = pl.BlockSpec(memory_space=pltpu.VMEM)


def on_device(parcels, cell_index, counts, coupling):
    inputs = [pltpu.with_memory_space_constraint(v, pltpu.HBM) for v in (parcels[0, 0], cell_index[0, 0], counts[0], coupling)]
    return pl.pallas_call(
        whole_kernel,
        out_shape=jax.ShapeDtypeStruct((COMP, CA, CY, NZ), F32),
        in_specs=[pl.BlockSpec(memory_space=pltpu.HBM)] * 4,
        out_specs=VMEM_SPEC,
        scratch_shapes=[
            pltpu.VMEM((64, 16, 64), BF),
            pltpu.VMEM((64, 64), jnp.int32),
            pltpu.VMEM((1, 64), jnp.int32),
            pltpu.VMEM((COMP, 16), BF),
            pltpu.VMEM((8, 32, 128), BF),
            pltpu.VMEM((8, 32, 128), BF),
            pltpu.VMEM((8, 32, 128), BF),
            pltpu.VMEM((3, 8, 32, 128), BF),
            pltpu.VMEM((3, 8, SLOTS), F32),
            pltpu.VMEM((3, CY, SLOTS), F32),
            pltpu.VMEM((3, FZ, SLOTS), BF),
            pltpu.VMEM((2, 2, 256, SLOTS), BF),
            pltpu.VMEM((2, 512, FZ), F32),
            pltpu.VMEM((2, 2, 2, 256, 256), F32),
            pltpu.VMEM((2, 256, 256), F32),
            pltpu.VMEM((2, 2, 2, 16, 16, 256), BF),
            pltpu.VMEM((2, 2, 2, 16, 16, 256), BF),
            pltpu.VMEM((256, 512), BF),
            pltpu.VMEM((128, 256), BF),
            pltpu.VMEM((256, NZ), BF),
            pltpu.VMEM((CA, NZ), F32),
            pltpu.VMEM((CY, NZ), F32),
            pltpu.SemaphoreType.DMA((4,)),
            pltpu.SemaphoreType.DMA((7,)),
            pltpu.SemaphoreType.DMA((7,)),
            pltpu.SemaphoreType.DMA((7,)),
            pltpu.SemaphoreType.DMA((7,)),
            pltpu.SemaphoreType.DMA((2, 2)),
            pltpu.SemaphoreType.DMA((2, 2)),
            pltpu.SemaphoreType.DMA((8,)),
            pltpu.SemaphoreType.DMA((8,)),
        ],
        compiler_params=pltpu.CompilerParams(vmem_limit_bytes=40 << 20, collective_id=0, has_side_effects=True),
        name="deposit_and_smooth",
    )(*inputs)


def solution(mesh):
    return jax.shard_map(
        on_device,
        mesh=mesh,
        in_specs=(
            P("ax", "cr", None, None, None),
            P("ax", "cr", None, None),
            P("ax", "cr", None),
            P(),
        ),
        out_specs=P(None, "ax", "cr", None),
        check_vma=False,
    )
```

```python
import math

import jax
import jax.numpy as jnp
import ml_dtypes
import numpy as np
from jax import lax
from jax.experimental import pallas as pl
from jax.experimental.pallas import tpu as pltpu
from jax.sharding import PartitionSpec as P

CA = 32
CY = 32
NZ = 128
COMP = 4
HALF = 16
NX = 384
NY = 2048
SLOTS = 4096
FZ = COMP * NZ
BF = jnp.bfloat16
F32 = jnp.float32
NT = (((1,), (1,)), ((), ()))

VOLUME = 256.0
SIGMA = 0.75 * HALF
TAPS = [math.exp(-k * k / (2.0 * SIGMA * SIGMA)) for k in range(HALF + 1)]
STRETCH = 1.8433
HELD = [float(np.float32(STRETCH * t).astype(ml_dtypes.bfloat16)) for t in TAPS]
_W = [1.0] + [2.0] * HALF
UNDO = sum(w * h * t for w, h, t in zip(_W, HELD, TAPS)) / sum(w * h * h for w, h in zip(_W, HELD))


ROWS = 16


def iota(shape, axis):
    return lax.broadcasted_iota(jnp.int32, shape, axis)


def weight_sum(pos, extent):
    total = jnp.zeros(pos.shape, F32)
    for k in range(-HALF, HALF + 1):
        inside = (pos + k >= 0) & (pos + k < extent)
        total = total + jnp.where(inside, TAPS[abs(k)], 0.0)
    return total


def taps_at(gap, where):
    value = jnp.zeros(gap.shape, F32)
    for k in range(HALF + 1):
        value = jnp.where(gap == k, HELD[k], value)
    return jnp.where(where, value, 0.0).astype(BF)


def axial_band(below, above):
    r, s = iota((256, 512), 0), iota((256, 512), 1)
    own, low = s < 256, s < 384
    row = jnp.where(own, s >> 5, (s >> 4) & 7)
    layer = jnp.where(own, s & 31, jnp.where(low, (s & 15) - 16, (s & 15) + 32))
    there = own | (jnp.where(low, below, above) > 0)
    return taps_at(jnp.abs((r >> 3) - layer), ((r & 7) == row) & there)


def cross_band(below, above):
    r, s = iota((128, 256), 0), iota((128, 256), 1)
    part = s >> 5
    row = (s & 7) + part * 8 - jnp.where(part < 4, 0, jnp.where(part < 6, 48, 16))
    there = (part < 4) | (jnp.where(part < 6, below, above) > 0)
    return taps_at(jnp.abs((r & 31) - row), ((r >> 5) == ((s >> 3) & 3)) & there)


def depth_band():
    r, s = iota((256, NZ), 0), iota((256, NZ), 1)
    return taps_at(jnp.abs((r & 127) - s), s >= 0)


def split(v):
    high = v.astype(BF)
    return high, (v - high.astype(F32)).astype(BF)


def whole_kernel(
    parcels_hbm, cell_hbm, counts_hbm, coupling_hbm, out_ref,
    parcels_ref, cell_ref, counts_ref, coupling_ref, msg1, buf1, msg2, lists, flat, keys, wt, picks, acc_own, axial, acc_side, e_own, e_side, kxs, kys, kzs, sx, syz, load,
    send1, recv1, send2, recv2, send_ax, recv_ax, send_cr, recv_cr,
):
    a, c_at = lax.axis_index("ax"), lax.axis_index("cr")
    n_ax, n_cr = lax.axis_size("ax"), lax.axis_size("cr")
    y_at, g_at = c_at // 8, c_at % 8
    up, down = lax.rem(a + 1, n_ax), lax.rem(a + n_ax - 1, n_ax)
    right, left = lax.rem(c_at + 1, n_cr), lax.rem(c_at + n_cr - 1, n_cr)
    in_row = [(a, y_at * 8 + lax.rem(g_at + j, 8)) for j in range(1, 8)]
    in_column = [(a, lax.rem(y_at + j, 8) * 8 + g_at) for j in range(1, 8)]

    def remote(src, dst, send, recv, to):
        return pltpu.make_async_remote_copy(
            src_ref=src, dst_ref=dst, send_sem=send, recv_sem=recv, device_id=to, device_id_type=pl.DeviceIdType.MESH
        )

    loads = [
        pltpu.make_async_copy(src, dst, load.at[k])
        for k, (src, dst) in enumerate(
            [(parcels_hbm, parcels_ref), (cell_hbm, cell_ref), (counts_hbm, counts_ref), (coupling_hbm, coupling_ref)]
        )
    ]
    for copy in loads:
        copy.start()
    barrier = pltpu.get_barrier_semaphore()
    partners = in_row + in_column + [(up, c_at), (down, c_at), (a, right), (a, left)]
    for to in partners:
        pl.semaphore_signal(barrier, inc=1, device_id=to, device_id_type=pl.DeviceIdType.MESH)

    one, zero = jnp.ones((), BF), jnp.zeros((), BF)
    for copy in loads:
        copy.wait()

    r, s = iota((128, 4), 0), iota((128, 4), 1)
    spread = jnp.dot(((r & 7) == s).astype(F32).astype(BF), coupling_ref[...], preferred_element_type=F32).astype(BF)
    r, s = iota((16, 256), 0), iota((16, 256), 1)
    spread = jnp.dot(spread, ((s & 15) == r).astype(F32).astype(BF), preferred_element_type=F32)
    r, s = iota((128, 256), 0), iota((128, 256), 1)
    mix = jnp.where((r >> 3) == (s >> 4), spread, 0.0).astype(BF)
    eye = (iota((64, 64), 0) == iota((64, 64), 1)).astype(F32).astype(BF)
    counts = jnp.broadcast_to(counts_ref[...].astype(F32), (64, 64)).astype(BF)
    counts = lax.dot_general(eye, counts, NT, preferred_element_type=F32)
    live = iota((64, 64), 1).astype(F32) < counts
    cell = cell_ref[...]
    codes = []
    for code in (jnp.where(live, cell & 127, -1), (cell >> 7) & 31, cell >> 12):
        code = code.astype(F32)
        codes.append(jnp.concatenate([code[:32], code[32:]], axis=1))
    codes = jnp.concatenate(codes, axis=0).astype(BF)
    for group in range(2):
        records = []
        for b in range(16):
            d = (b % 4) * 8 + 4 * group + b // 4
            records.append(jnp.concatenate([parcels_ref[d], parcels_ref[d + 32]], axis=1))
        letter = jnp.dot(mix, jnp.concatenate(records, axis=0), preferred_element_type=F32)
        r, s = iota((128, 96), 0), iota((128, 96), 1)
        b = r >> 3
        choose = ((r & 7) == 4 + (s >> 5)) & ((s & 31) == (b & 3) * 8 + 4 * group + (b >> 2))
        letter += jnp.dot(choose.astype(F32).astype(BF), codes, preferred_element_type=F32)
        msg1[group * 4 : group * 4 + 4] = letter.astype(BF).reshape(4, 32, 128)

    pl.semaphore_wait(barrier, len(partners))
    first = []
    for j in range(1, 8):
        first.append(remote(msg1.at[lax.rem(g_at + j, 8)], buf1.at[g_at], send1.at[j - 1], recv1.at[j - 1], in_row[j - 1]))
        first[-1].start()
    buf1[g_at] = msg1[g_at]

    kxs[...] = axial_band(a, n_ax - 1 - a)
    kys[...] = cross_band(c_at, n_cr - 1 - c_at)
    kzs[...] = depth_band()
    sx[...] = 1.0 / weight_sum(iota((CA, NZ), 0) + a * CA, NX)
    syz[...] = (VOLUME * UNDO**3) / (
        weight_sum(iota((CY, NZ), 0) + c_at * CY, NY) * weight_sum(iota((8, NZ), 1), NZ)[0:1, :]
    )

    for copy in first:
        copy.wait_recv()
    near = iota((32, 128), 1) < 64
    halves = []
    for m in range(4):
        p, q = buf1[2 * m].astype(F32), buf1[2 * m + 1].astype(F32)
        halves.append((jnp.where(near, p, pltpu.roll(q, 64, 1)), jnp.where(near, pltpu.roll(p, 64, 1), q)))
    for h in range(2):
        for i in range(4):
            msg2[4 * h + i] = jnp.concatenate([halves[m][h][i * 8 : i * 8 + 8] for m in range(4)], axis=0).astype(BF)
    place = {j: p for p, j in enumerate((0, 1, 7, 2, 6, 3, 5, 4))}
    second = {}
    for j in (4, 3, 5, 2, 6, 1, 7):
        second[j] = remote(
            msg2.at[lax.rem(y_at + j, 8)], lists.at[0, place[j]], send2.at[j - 1], recv2.at[j - 1], in_column[j - 1]
        )
        second[j].start()
    lists[0, 0] = msg2[y_at]

    def rows_iota(n, width):
        return iota((n, width), 0).astype(F32).astype(BF)

    def unfold(l, p):
        ks = slice(p * 512, p * 512 + 512)
        rows = lists[l, p].astype(F32)
        flat[l, :, ks] = jnp.concatenate([rows[b * 8 : b * 8 + 8] for b in range(4)], axis=1)
        hit = jnp.broadcast_to(flat[l, 4:5, ks].astype(BF), (NZ, 512)) == rows_iota(NZ, 512)
        for f in range(COMP):
            term = jnp.broadcast_to(flat[l, f : f + 1, ks].astype(BF), (NZ, 512))
            wt[l, f * NZ : (f + 1) * NZ, ks] = jnp.where(hit, term, zero)
        n, x0 = (32, 0) if l == 0 else (16, 16 if l == 1 else 0)
        y = jnp.broadcast_to(flat[l, 5:6, ks], (CY, 512))
        x = jnp.broadcast_to(flat[l, 6:7, ks], (CY, 512)) - float(x0)
        here = (y == iota((CY, 512), 0).astype(F32)) & (x >= 0) & (x < n)
        keys[l, :, ks] = jnp.where(here, x, -1.0)

    def picked(l, rows, ks, width):
        n = 32 if l == 0 else 16
        parts = []
        for i in rows:
            key = jnp.broadcast_to(keys[l, i : i + 1, ks].astype(BF), (n, width))
            parts.append(jnp.where(key == rows_iota(n, width), one, zero))
        return jnp.concatenate(parts, axis=0)

    def deposit(first_place, last_place):
        for p in range(first_place, last_place):
            unfold(0, p)
        ks = slice(first_place * 512, last_place * 512)
        for c in range(2):
            rows = range(c * ROWS, c * ROWS + ROWS)
            d = lax.dot_general(
                picked(0, rows, ks, ks.stop - ks.start), wt[0, :, ks], NT, preferred_element_type=F32
            )
            acc_own[c] = d if first_place == 0 else acc_own[c] + d

    along = {}

    def hand_on(part, first_place, last_place):
        ps = pl.ds(first_place, last_place - first_place)
        for k, to in ((0, up), (1, down)):
            along[k, part] = remote(
                lists.at[0, ps], lists.at[1 + k, ps], send_ax.at[k, part], recv_ax.at[k, part], (to, c_at)
            )
            along[k, part].start()

    deposit(0, 1)
    for j in (1, 7):
        second[j].wait_recv()
    hand_on(0, 0, 3)
    deposit(1, 3)
    for j in (2, 6, 3, 5, 4):
        second[j].wait_recv()
    hand_on(1, 3, 8)
    deposit(3, 8)
    for h in range(2):
        for i in range(2):
            for c in range(2):
                high, low = split(acc_own[c, i * 256 : i * 256 + 256, h * 256 : h * 256 + 256])
                v = jnp.dot(kxs[:, :256], high, preferred_element_type=F32)
                v += jnp.dot(kxs[:, :256], low, preferred_element_type=F32)
                axial[h, i, c] = v
    for part, places in enumerate((range(3), range(3, 8))):
        for l in (1, 2):
            along[l - 1, part].wait_recv()
            for p in places:
                unfold(l, p)
    for l in (1, 2):
        for i in range(2):
            rows = [c * ROWS + i * 8 + k for c in range(2) for k in range(8)]
            picks[l - 1, i * 256 : i * 256 + 256] = picked(l, rows, slice(0, SLOTS), SLOTS)
    across = []
    for h in range(2):
        fs = slice(h * 256, h * 256 + 256)
        for i in range(2):
            part = slice(i * 256, i * 256 + 256) if h else slice(0, 512)
            for l in (1, 2) if h or i == 0 else ():
                acc_side[l - 1, part] = lax.dot_general(
                    picks[l - 1, part], wt[l, fs, :], NT, preferred_element_type=F32
                )
            for c in range(2):
                sides = [acc_side[k, i * 256 + c * 128 : i * 256 + c * 128 + 128, :] for k in range(2)]
                high, low = split(jnp.concatenate(sides, axis=0))
                v = jnp.dot(kxs[:, 256:], high, preferred_element_type=F32)
                v += jnp.dot(kxs[:, 256:], low, preferred_element_type=F32)
                v += axial[h, i, c]
                e_own[h, i, c] = v.astype(BF).reshape(16, 16, 256)
                k = h * 4 + i * 2 + c
                across.append(
                    remote(e_own.at[h, i, c], e_side.at[h, i, 1 - c], send_cr.at[k], recv_cr.at[k], (a, (left, right)[c]))
                )
                across[-1].start()
    for h in range(2):
        for copy in across[4 * h : 4 * h + 4]:
            copy.wait_recv()
        for start in range(0, CA // 4, 8):
            crossed = []
            for g in range(start, start + 8):
                xs = slice(g * 2, g * 2 + 2)
                rhs = [e[h, i, c, xs].reshape(32, 256) for e in (e_own, e_side) for c in range(2) for i in range(2)]
                crossed.append(jnp.dot(kys[...], jnp.concatenate(rhs, axis=0), preferred_element_type=F32))
            for f in range(2):
                high, low = split(jnp.concatenate([v[:, f * 128 : f * 128 + 128] for v in crossed], axis=0))
                v = jnp.dot(jnp.concatenate([high, low], axis=1), kzs[...], preferred_element_type=F32)
                v = v.reshape(32, CY, NZ)
                for i in range(32):
                    x = start * 4 + i
                    out_ref[2 * h + f, x] = v[i] * (syz[...] * sx[x : x + 1, :])
    for copy in first + list(second.values()) + list(along.values()) + across:
        copy.wait_send()


VMEM_SPEC = pl.BlockSpec(memory_space=pltpu.VMEM)


def on_device(parcels, cell_index, counts, coupling):
    inputs = [pltpu.with_memory_space_constraint(v, pltpu.HBM) for v in (parcels[0, 0], cell_index[0, 0], counts[0], coupling)]
    return pl.pallas_call(
        whole_kernel,
        out_shape=jax.ShapeDtypeStruct((COMP, CA, CY, NZ), F32),
        in_specs=[pl.BlockSpec(memory_space=pltpu.HBM)] * 4,
        out_specs=VMEM_SPEC,
        scratch_shapes=[
            pltpu.VMEM((64, 16, 64), BF),
            pltpu.VMEM((64, 64), jnp.int32),
            pltpu.VMEM((1, 64), jnp.int32),
            pltpu.VMEM((COMP, 16), BF),
            pltpu.VMEM((8, 32, 128), BF),
            pltpu.VMEM((8, 32, 128), BF),
            pltpu.VMEM((8, 32, 128), BF),
            pltpu.VMEM((3, 8, 32, 128), BF),
            pltpu.VMEM((3, 8, SLOTS), F32),
            pltpu.VMEM((3, CY, SLOTS), F32),
            pltpu.VMEM((3, FZ, SLOTS), BF),
            pltpu.VMEM((2, 512, SLOTS), BF),
            pltpu.VMEM((2, 512, FZ), F32),
            pltpu.VMEM((2, 2, 2, 256, 256), F32),
            pltpu.VMEM((2, 512, 256), F32),
            pltpu.VMEM((2, 2, 2, 16, 16, 256), BF),
            pltpu.VMEM((2, 2, 2, 16, 16, 256), BF),
            pltpu.VMEM((256, 512), BF),
            pltpu.VMEM((128, 256), BF),
            pltpu.VMEM((256, NZ), BF),
            pltpu.VMEM((CA, NZ), F32),
            pltpu.VMEM((CY, NZ), F32),
            pltpu.SemaphoreType.DMA((4,)),
            pltpu.SemaphoreType.DMA((7,)),
            pltpu.SemaphoreType.DMA((7,)),
            pltpu.SemaphoreType.DMA((7,)),
            pltpu.SemaphoreType.DMA((7,)),
            pltpu.SemaphoreType.DMA((2, 2)),
            pltpu.SemaphoreType.DMA((2, 2)),
            pltpu.SemaphoreType.DMA((8,)),
            pltpu.SemaphoreType.DMA((8,)),
        ],
        compiler_params=pltpu.CompilerParams(vmem_limit_bytes=40 << 20, collective_id=0, has_side_effects=True),
        name="deposit_and_smooth",
    )(*inputs)


def solution(mesh):
    return jax.shard_map(
        on_device,
        mesh=mesh,
        in_specs=(
            P("ax", "cr", None, None, None),
            P("ax", "cr", None, None),
            P("ax", "cr", None),
            P(),
        ),
        out_specs=P(None, "ax", "cr", None),
        check_vma=False,
    )
```

```python
import math

import jax
import jax.numpy as jnp
import ml_dtypes
import numpy as np
from jax import lax
from jax.experimental import pallas as pl
from jax.experimental.pallas import tpu as pltpu
from jax.sharding import PartitionSpec as P

CA = 32
CY = 32
NZ = 128
COMP = 4
HALF = 16
NX = 384
NY = 2048
SLOTS = 4096
FZ = COMP * NZ
BF = jnp.bfloat16
F32 = jnp.float32
NT = (((1,), (1,)), ((), ()))

VOLUME = 256.0
SIGMA = 0.75 * HALF
TAPS = [math.exp(-k * k / (2.0 * SIGMA * SIGMA)) for k in range(HALF + 1)]
STRETCH = 1.8433
HELD = [float(np.float32(STRETCH * t).astype(ml_dtypes.bfloat16)) for t in TAPS]
_W = [1.0] + [2.0] * HALF
UNDO = sum(w * h * t for w, h, t in zip(_W, HELD, TAPS)) / sum(w * h * h for w, h in zip(_W, HELD))


ROWS = 16


def iota(shape, axis):
    return lax.broadcasted_iota(jnp.int32, shape, axis)


def weight_sum(pos, extent):
    total = jnp.zeros(pos.shape, F32)
    for k in range(-HALF, HALF + 1):
        inside = (pos + k >= 0) & (pos + k < extent)
        total = total + jnp.where(inside, TAPS[abs(k)], 0.0)
    return total


def taps_at(gap, where):
    value = jnp.zeros(gap.shape, F32)
    for k in range(HALF + 1):
        value = jnp.where(gap == k, HELD[k], value)
    return jnp.where(where, value, 0.0).astype(BF)


def axial_band(below, above):
    r, s = iota((256, 512), 0), iota((256, 512), 1)
    own, low = s < 256, s < 384
    row = jnp.where(own, s >> 5, (s >> 4) & 7)
    layer = jnp.where(own, s & 31, jnp.where(low, (s & 15) - 16, (s & 15) + 32))
    there = own | (jnp.where(low, below, above) > 0)
    return taps_at(jnp.abs((r >> 3) - layer), ((r & 7) == row) & there)


def cross_band(below, above):
    r, s = iota((128, 256), 0), iota((128, 256), 1)
    part = s >> 5
    row = (s & 7) + part * 8 - jnp.where(part < 4, 0, jnp.where(part < 6, 48, 16))
    there = (part < 4) | (jnp.where(part < 6, below, above) > 0)
    return taps_at(jnp.abs((r & 31) - row), ((r >> 5) == ((s >> 3) & 3)) & there)


def depth_band():
    r, s = iota((256, NZ), 0), iota((256, NZ), 1)
    return taps_at(jnp.abs((r & 127) - s), s >= 0)


def split(v):
    high = v.astype(BF)
    return high, (v - high.astype(F32)).astype(BF)


def whole_kernel(
    parcels_hbm, cell_hbm, counts_hbm, coupling_hbm, out_ref,
    parcels_ref, cell_ref, counts_ref, coupling_ref, msg1, buf1, msg2, lists, flat, keys, wt, picks, acc_own, axial, acc_side, e_own, e_side, kxs, kys, kzs, sx, syz, load,
    send1, recv1, send2, recv2, send_ax, recv_ax, send_cr, recv_cr,
):
    a, c_at = lax.axis_index("ax"), lax.axis_index("cr")
    n_ax, n_cr = lax.axis_size("ax"), lax.axis_size("cr")
    y_at, g_at = c_at // 8, c_at % 8
    up, down = lax.rem(a + 1, n_ax), lax.rem(a + n_ax - 1, n_ax)
    right, left = lax.rem(c_at + 1, n_cr), lax.rem(c_at + n_cr - 1, n_cr)
    in_row = [(a, y_at * 8 + lax.rem(g_at + j, 8)) for j in range(1, 8)]
    in_column = [(a, lax.rem(y_at + j, 8) * 8 + g_at) for j in range(1, 8)]

    def remote(src, dst, send, recv, to):
        return pltpu.make_async_remote_copy(
            src_ref=src, dst_ref=dst, send_sem=send, recv_sem=recv, device_id=to, device_id_type=pl.DeviceIdType.MESH
        )

    loads = [
        pltpu.make_async_copy(src, dst, load.at[k])
        for k, (src, dst) in enumerate(
            [(parcels_hbm, parcels_ref), (cell_hbm, cell_ref), (counts_hbm, counts_ref), (coupling_hbm, coupling_ref)]
        )
    ]
    for copy in loads:
        copy.start()
    barrier = pltpu.get_barrier_semaphore()
    partners = in_row + in_column + [(up, c_at), (down, c_at), (a, right), (a, left)]
    for to in partners:
        pl.semaphore_signal(barrier, inc=1, device_id=to, device_id_type=pl.DeviceIdType.MESH)

    one, zero = jnp.ones((), BF), jnp.zeros((), BF)
    for copy in loads:
        copy.wait()

    r, s = iota((128, 4), 0), iota((128, 4), 1)
    spread = jnp.dot(((r & 7) == s).astype(F32).astype(BF), coupling_ref[...], preferred_element_type=F32).astype(BF)
    r, s = iota((16, 256), 0), iota((16, 256), 1)
    spread = jnp.dot(spread, ((s & 15) == r).astype(F32).astype(BF), preferred_element_type=F32)
    r, s = iota((128, 256), 0), iota((128, 256), 1)
    mix = jnp.where((r >> 3) == (s >> 4), spread, 0.0).astype(BF)
    eye = (iota((64, 64), 0) == iota((64, 64), 1)).astype(F32).astype(BF)
    counts = jnp.broadcast_to(counts_ref[...].astype(F32), (64, 64)).astype(BF)
    counts = lax.dot_general(eye, counts, NT, preferred_element_type=F32)
    live = iota((64, 64), 1).astype(F32) < counts
    cell = cell_ref[...]
    codes = []
    for code in (jnp.where(live, cell & 127, -1), (cell >> 7) & 31, cell >> 12):
        code = code.astype(F32)
        codes.append(jnp.concatenate([code[:32], code[32:]], axis=1))
    codes = jnp.concatenate(codes, axis=0).astype(BF)
    for group in range(2):
        records = []
        for b in range(16):
            d = (b % 4) * 8 + 4 * group + b // 4
            records.append(jnp.concatenate([parcels_ref[d], parcels_ref[d + 32]], axis=1))
        letter = jnp.dot(mix, jnp.concatenate(records, axis=0), preferred_element_type=F32)
        r, s = iota((128, 96), 0), iota((128, 96), 1)
        b = r >> 3
        choose = ((r & 7) == 4 + (s >> 5)) & ((s & 31) == (b & 3) * 8 + 4 * group + (b >> 2))
        letter += jnp.dot(choose.astype(F32).astype(BF), codes, preferred_element_type=F32)
        msg1[group * 4 : group * 4 + 4] = letter.astype(BF).reshape(4, 32, 128)

    pl.semaphore_wait(barrier, len(partners))
    first = []
    for j in range(1, 8):
        first.append(remote(msg1.at[lax.rem(g_at + j, 8)], buf1.at[g_at], send1.at[j - 1], recv1.at[j - 1], in_row[j - 1]))
        first[-1].start()
    buf1[g_at] = msg1[g_at]

    kxs[...] = axial_band(a, n_ax - 1 - a)
    kys[...] = cross_band(c_at, n_cr - 1 - c_at)
    kzs[...] = depth_band()
    sx[...] = 1.0 / weight_sum(iota((CA, NZ), 0) + a * CA, NX)
    syz[...] = (VOLUME * UNDO**3) / (
        weight_sum(iota((CY, NZ), 0) + c_at * CY, NY) * weight_sum(iota((8, NZ), 1), NZ)[0:1, :]
    )

    for copy in first:
        copy.wait_recv()
    near = iota((32, 128), 1) < 64
    halves = []
    for m in range(4):
        p, q = buf1[2 * m].astype(F32), buf1[2 * m + 1].astype(F32)
        halves.append((jnp.where(near, p, pltpu.roll(q, 64, 1)), jnp.where(near, pltpu.roll(p, 64, 1), q)))
    for h in range(2):
        for i in range(4):
            msg2[4 * h + i] = jnp.concatenate([halves[m][h][i * 8 : i * 8 + 8] for m in range(4)], axis=0).astype(BF)
    place = {j: p for p, j in enumerate((0, 1, 7, 2, 6, 3, 5, 4))}
    second = {}
    for j in (4, 3, 5, 2, 6, 1, 7):
        second[j] = remote(
            msg2.at[lax.rem(y_at + j, 8)], lists.at[0, place[j]], send2.at[j - 1], recv2.at[j - 1], in_column[j - 1]
        )
        second[j].start()
    lists[0, 0] = msg2[y_at]

    def rows_iota(n, width):
        return iota((n, width), 0).astype(F32).astype(BF)

    def unfold(l, p):
        ks = slice(p * 512, p * 512 + 512)
        rows = lists[l, p].astype(F32)
        flat[l, :, ks] = jnp.concatenate([rows[b * 8 : b * 8 + 8] for b in range(4)], axis=1)
        hit = jnp.broadcast_to(flat[l, 4:5, ks].astype(BF), (NZ, 512)) == rows_iota(NZ, 512)
        for f in range(COMP):
            term = jnp.broadcast_to(flat[l, f : f + 1, ks].astype(BF), (NZ, 512))
            wt[l, f * NZ : (f + 1) * NZ, ks] = jnp.where(hit, term, zero)
        n, x0 = (32, 0) if l == 0 else (16, 16 if l == 1 else 0)
        y = jnp.broadcast_to(flat[l, 5:6, ks], (CY, 512))
        x = jnp.broadcast_to(flat[l, 6:7, ks], (CY, 512)) - float(x0)
        here = (y == iota((CY, 512), 0).astype(F32)) & (x >= 0) & (x < n)
        keys[l, :, ks] = jnp.where(here, x, -1.0)

    def picked(l, rows, ks, width):
        n = 32 if l == 0 else 16
        parts = []
        for i in rows:
            key = jnp.broadcast_to(keys[l, i : i + 1, ks].astype(BF), (n, width))
            parts.append(jnp.where(key == rows_iota(n, width), one, zero))
        return jnp.concatenate(parts, axis=0)

    def deposit(first_place, last_place):
        for p in range(first_place, last_place):
            unfold(0, p)
        ks = slice(first_place * 512, last_place * 512)
        for c in range(2):
            rows = range(c * ROWS, c * ROWS + ROWS)
            d = lax.dot_general(
                picked(0, rows, ks, ks.stop - ks.start), wt[0, :, ks], NT, preferred_element_type=F32
            )
            acc_own[c] = d if first_place == 0 else acc_own[c] + d

    along = {}

    def hand_on(part, first_place, last_place):
        ps = pl.ds(first_place, last_place - first_place)
        for k, to in ((0, up), (1, down)):
            along[k, part] = remote(
                lists.at[0, ps], lists.at[1 + k, ps], send_ax.at[k, part], recv_ax.at[k, part], (to, c_at)
            )
            along[k, part].start()

    deposit(0, 1)
    for j in (1, 7):
        second[j].wait_recv()
    hand_on(0, 0, 3)
    deposit(1, 3)
    for j in (2, 6, 3, 5, 4):
        second[j].wait_recv()
    hand_on(1, 3, 8)
    deposit(3, 8)
    for h in range(2):
        for i in range(2):
            for c in range(2):
                high, low = split(acc_own[c, i * 256 : i * 256 + 256, h * 256 : h * 256 + 256])
                v = jnp.dot(kxs[:, :256], high, preferred_element_type=F32)
                v += jnp.dot(kxs[:, :256], low, preferred_element_type=F32)
                axial[h, i, c] = v
    for part, places in enumerate((range(3), range(3, 8))):
        for l in (1, 2):
            along[l - 1, part].wait_recv()
            for p in places:
                unfold(l, p)
    across = []
    for h in range(2):
        fs = slice(h * 256, h * 256 + 256)
        for i in range(2):
            for l in (1, 2):
                if h == 0:
                    rows = [c * ROWS + i * 8 + k for c in range(2) for k in range(8)]
                    picks[i, l - 1] = picked(l, rows, slice(0, SLOTS), SLOTS)
                acc_side[l - 1] = lax.dot_general(picks[i, l - 1], wt[l, fs, :], NT, preferred_element_type=F32)
            for c in range(2):
                sides = [acc_side[k, c * 128 : c * 128 + 128, :] for k in range(2)]
                high, low = split(jnp.concatenate(sides, axis=0))
                v = jnp.dot(kxs[:, 256:], high, preferred_element_type=F32)
                v += jnp.dot(kxs[:, 256:], low, preferred_element_type=F32)
                v += axial[h, i, c]
                e_own[h, i, c] = v.astype(BF).reshape(16, 16, 256)
                k = h * 4 + i * 2 + c
                across.append(
                    remote(e_own.at[h, i, c], e_side.at[h, i, 1 - c], send_cr.at[k], recv_cr.at[k], (a, (left, right)[c]))
                )
                across[-1].start()
    for h in range(2):
        for copy in across[4 * h : 4 * h + 4]:
            copy.wait_recv()
        for start in range(0, CA // 4, 8):
            crossed = []
            for g in range(start, start + 8):
                xs = slice(g * 2, g * 2 + 2)
                rhs = [e[h, i, c, xs].reshape(32, 256) for e in (e_own, e_side) for c in range(2) for i in range(2)]
                crossed.append(jnp.dot(kys[...], jnp.concatenate(rhs, axis=0), preferred_element_type=F32))
            for f in range(2):
                high, low = split(jnp.concatenate([v[:, f * 128 : f * 128 + 128] for v in crossed], axis=0))
                v = jnp.dot(jnp.concatenate([high, low], axis=1), kzs[...], preferred_element_type=F32)
                v = v.reshape(32, CY, NZ)
                for i in range(32):
                    x = start * 4 + i
                    out_ref[2 * h + f, x] = v[i] * (syz[...] * sx[x : x + 1, :])
    for copy in first + list(second.values()) + list(along.values()) + across:
        copy.wait_send()


VMEM_SPEC = pl.BlockSpec(memory_space=pltpu.VMEM)


def on_device(parcels, cell_index, counts, coupling):
    inputs = [pltpu.with_memory_space_constraint(v, pltpu.HBM) for v in (parcels[0, 0], cell_index[0, 0], counts[0], coupling)]
    return pl.pallas_call(
        whole_kernel,
        out_shape=jax.ShapeDtypeStruct((COMP, CA, CY, NZ), F32),
        in_specs=[pl.BlockSpec(memory_space=pltpu.HBM)] * 4,
        out_specs=VMEM_SPEC,
        scratch_shapes=[
            pltpu.VMEM((64, 16, 64), BF),
            pltpu.VMEM((64, 64), jnp.int32),
            pltpu.VMEM((1, 64), jnp.int32),
            pltpu.VMEM((COMP, 16), BF),
            pltpu.VMEM((8, 32, 128), BF),
            pltpu.VMEM((8, 32, 128), BF),
            pltpu.VMEM((8, 32, 128), BF),
            pltpu.VMEM((3, 8, 32, 128), BF),
            pltpu.VMEM((3, 8, SLOTS), F32),
            pltpu.VMEM((3, CY, SLOTS), F32),
            pltpu.VMEM((3, FZ, SLOTS), BF),
            pltpu.VMEM((2, 2, 256, SLOTS), BF),
            pltpu.VMEM((2, 512, FZ), F32),
            pltpu.VMEM((2, 2, 2, 256, 256), F32),
            pltpu.VMEM((2, 256, 256), F32),
            pltpu.VMEM((2, 2, 2, 16, 16, 256), BF),
            pltpu.VMEM((2, 2, 2, 16, 16, 256), BF),
            pltpu.VMEM((256, 512), BF),
            pltpu.VMEM((128, 256), BF),
            pltpu.VMEM((256, NZ), BF),
            pltpu.VMEM((CA, NZ), F32),
            pltpu.VMEM((CY, NZ), F32),
            pltpu.SemaphoreType.DMA((4,)),
            pltpu.SemaphoreType.DMA((7,)),
            pltpu.SemaphoreType.DMA((7,)),
            pltpu.SemaphoreType.DMA((7,)),
            pltpu.SemaphoreType.DMA((7,)),
            pltpu.SemaphoreType.DMA((2, 2)),
            pltpu.SemaphoreType.DMA((2, 2)),
            pltpu.SemaphoreType.DMA((8,)),
            pltpu.SemaphoreType.DMA((8,)),
        ],
        compiler_params=pltpu.CompilerParams(vmem_limit_bytes=40 << 20, collective_id=0, has_side_effects=True),
        name="deposit_and_smooth",
    )(*inputs)


def solution(mesh):
    return jax.shard_map(
        on_device,
        mesh=mesh,
        in_specs=(
            P("ax", "cr", None, None, None),
            P("ax", "cr", None, None),
            P("ax", "cr", None),
            P(),
        ),
        out_specs=P(None, "ax", "cr", None),
        check_vma=False,
    )
```
